512 devices in a mesh: tm: 128 (over z, y, core), chan: 4 (over x).
Axes of the slice: x: 4, y: 4, z: 16, core: 2. Of those that a mesh axis runs over, the one named last changes fastest.
Arguments:
- video: bfloat16 [512, 128, 512], P('tm', 'chan'), may hold values from -6 to 6
- clip_start: int32 [512], P('tm'), may hold values from 0 to 511, as said below
- first_conv_weight: bfloat16 [3, 128, 256], P(None, None, 'chan'), may hold values from -0.3125 to 0.3125
- second_conv_weight: bfloat16 [3, 256, 512], P(None, None, 'chan'), may hold values from -0.21875 to 0.21875
- cotangent: bfloat16 [256, 512, 512], P('tm', 'chan'), may hold values from -6 to 6
Outputs:
- encoded: bfloat16 [256, 512, 512], P('tm', 'chan')
- first_weight_gradient: float32 [3, 128, 256], P(None, None, 'chan')
- second_weight_gradient: float32 [3, 256, 512], P(None, None, 'chan')
The draws below stay inside these ranges and needn't reach their ends.
Inputs may be any that keep to these rules, and one draw needn't show every extreme that they name: clip_start[0] = 0, clip_start[t] <= t, it never falls, and clip_start[clip_start[t]] = clip_start[t]; the last frame starts a clip of its own; clips have mixed lengths.
All inputs are finite; a program needn't handle non-finite values.
Results may differ from the reference program's by a relative error of at most 0.0049.
Values may be sent and summed in bfloat16 or wider, within the bound.
A program may use at most 64 MiB of HBM per device.

```python
import jax
import jax.numpy as jnp
from jax import lax

C = 128
C2 = 256
C3 = 512
S = 512
FRAMES = 512
HALF = 256


def draw_clip_start(key, part):
    key = jax.random.fold_in(key, 11)
    frame_index = jnp.arange(FRAMES, dtype=jnp.int32)
    rolls = jax.random.randint(key, (FRAMES,), 0, 12)
    starts = (rolls == 0) | (frame_index == 0) | (frame_index == FRAMES - 1)
    marks = jnp.where(starts, frame_index, 0).astype(jnp.int32)
    return lax.cummax(marks, axis=0)


def shard_levels(rng, extent, split, low, top_value):
    loudness = 1.0
    for position, parts in split:
        draws = jax.random.uniform(jax.random.fold_in(jax.random.fold_in(rng, 6), position), (parts,), jnp.float32, low / len(split), top_value / len(split))
        loudness = loudness * jnp.repeat(jnp.exp(draws), extent[position] // parts).reshape((-1,) + (1,) * (len(extent) - 1 - position))
    return loudness


def gaussian(own_key, extent, scale, most, shards=(), held_as=jnp.bfloat16):
    drawn = scale * jax.random.normal(own_key, extent, jnp.float32)
    if shards:
        drawn = drawn * shard_levels(own_key, extent, shards, -0.22, 0.18)
    return jnp.clip(drawn, -most, most).astype(held_as)


def setup_inputs(seed: int = 0) -> dict:
    streams_of = jax.random.split(jax.random.key(seed), 6)
    return {
        "video": gaussian(streams_of[0], (FRAMES, C, S), 1.0, 6.0, ((0, 128), (1, 4))),
        "clip_start": draw_clip_start(jax.random.fold_in(streams_of[5], 71), 0),
        "first_conv_weight": gaussian(streams_of[2], (3, C, C2), (3 * C) ** -0.5, 0.3125, ((2, 4),)),
        "second_conv_weight": gaussian(streams_of[3], (3, C2, C3), (3 * C2) ** -0.5, 0.21875, ((2, 4),)),
        "cotangent": gaussian(streams_of[4], (HALF, C3, S), 1.0, 6.0, ((0, 128), (1, 4))),
    }


def reference(video, clip_start, first_conv_weight, second_conv_weight, cotangent):
    frames = video.shape[0]
    halved = frames // 2
    positions = video.shape[2]
    tap_offsets = jnp.arange(3, dtype=jnp.int32)
    frame_index = jnp.arange(frames, dtype=jnp.int32)
    first_source = jnp.maximum(frame_index[:, None] - tap_offsets[None, :], clip_start[:, None])
    video_wide = video.astype(jnp.float32)
    first_kernel = first_conv_weight.astype(jnp.float32)
    second_kernel = second_conv_weight.astype(jnp.float32)
    pre_activation = jnp.zeros((frames, first_kernel.shape[2], positions), jnp.float32)
    for filter_tap in range(3):
        pre_activation = pre_activation + jnp.einsum("em,reu->rmu", first_kernel[filter_tap], video_wide[first_source[:, filter_tap]])
    sigmoid_pre = jax.nn.sigmoid(pre_activation)
    activated = pre_activation * sigmoid_pre
    downsampled = (0.5 * (activated[0::2] + activated[1::2])).astype(jnp.bfloat16)
    half_index = jnp.arange(halved, dtype=jnp.int32)
    start_two = clip_start[0::2] // 2
    second_source = jnp.maximum(half_index[:, None] - tap_offsets[None, :], start_two[:, None])
    downsampled_wide = downsampled.astype(jnp.float32)
    encoded = jnp.zeros((halved, second_kernel.shape[2], positions), jnp.float32)
    for filter_tap in range(3):
        encoded = encoded + jnp.einsum("em,reu->rmu", second_kernel[filter_tap], downsampled_wide[second_source[:, filter_tap]])
    encoded = encoded.astype(jnp.bfloat16)
    cotangent_wide = cotangent.astype(jnp.float32)
    unit_grads = jnp.zeros((halved, second_kernel.shape[1], positions), jnp.float32)
    for filter_tap in range(3):
        tap_contribution = jnp.einsum("jk,dkp->djp", second_kernel[filter_tap], cotangent_wide)
        unit_grads = unit_grads.at[second_source[:, filter_tap]].add(tap_contribution)
    delta = (0.5 * jnp.repeat(unit_grads, 2, axis=0) * sigmoid_pre * (1.0 + pre_activation * (1.0 - sigmoid_pre))).astype(jnp.bfloat16)
    delta_wide = delta.astype(jnp.float32)
    first_scale = (frames * positions) ** -0.5
    second_scale = (halved * positions) ** -0.5
    first_weight_gradient = jnp.stack([jnp.einsum("rdm,rym->dy", video_wide[first_source[:, filter_tap]], delta_wide) for filter_tap in range(3)]) * first_scale
    second_weight_gradient = jnp.stack([jnp.einsum("rdm,rym->dy", downsampled_wide[second_source[:, filter_tap]], cotangent_wide) for filter_tap in range(3)]) * second_scale
    return encoded, first_weight_gradient, second_weight_gradient
```

```python
import jax
import jax.numpy as jnp
from jax import lax
from jax.experimental import pallas as pl
from jax.experimental.pallas import tpu as pltpu
from jax.sharding import PartitionSpec as P


def passed_along(block, axis, distance):
    devices = range(lax.axis_size(axis))
    route = [(i - distance, i) for i in devices if i - distance in devices]
    return lax.ppermute(block, axis, route)


MESH = pl.DeviceIdType.MESH
NQ = 8
NZ = 16


def sum_kernel(p1_ref, p2_ref, o1_ref, o2_ref, part, send1, recv1, mine, recv2, gather, held, sa, ra, sb, rb, sc, rc, sd, rd):
    me = lax.axis_index("tm")
    chan = lax.axis_index("chan")
    z, q = me // NQ, lax.rem(me, NQ)

    def in_z(s):
        return (z * NQ + lax.rem(q + s, NQ), chan)

    def over_z(s):
        return (lax.rem(z + s, NZ) * NQ + q, chan)

    barrier = pltpu.get_barrier_semaphore()
    for s in range(1, NQ):
        pl.semaphore_signal(barrier, inc=1, device_id=in_z(s), device_id_type=MESH)
    for s in range(1, NZ):
        pl.semaphore_signal(barrier, inc=1, device_id=over_z(s), device_id_type=MESH)
    for i in range(6):
        part[i] = p2_ref[i * 128 : (i + 1) * 128, :]
    part[6] = p1_ref[0:128, :]
    part[7] = jnp.concatenate([p1_ref[128:192, :], jnp.zeros((64, 128), jnp.float32)], axis=0)
    send1[...] = part[...].astype(jnp.bfloat16)
    pl.semaphore_wait(barrier, NQ + NZ - 2)

    def exchange(n, src, dst, ssem, rsem, device):
        copies = []
        for s in range(1, n):
            copy = pltpu.make_async_remote_copy(
                src_ref=src(s), dst_ref=dst(s), send_sem=ssem.at[s], recv_sem=rsem.at[s],
                device_id=device(s), device_id_type=MESH,
            )
            copy.start()
            copies.append(copy)
        return copies

    first = exchange(NQ, lambda s: send1.at[lax.rem(q + s, NQ)], lambda s: recv1.at[s], sa, ra, in_z)
    total = part[q]
    for s in range(1, NQ):
        first[s - 1].wait_recv()
        total = total + recv1[s].astype(jnp.float32)
    mine[...] = total.reshape(NZ, 8, 128)
    second = exchange(NZ, lambda s: mine.at[lax.rem(z + s, NZ)], lambda s: recv2.at[s], sb, rb, over_z)
    total = mine[z]
    for s in range(1, NZ):
        second[s - 1].wait_recv()
        total = total + recv2[s]
    gather[z] = total
    third = exchange(NZ, lambda s: gather.at[z], lambda s: gather.at[z], sc, rc, over_z)
    for copy in third:
        copy.wait_recv()
    held[q] = gather[...].reshape(128, 128).astype(jnp.bfloat16)
    fourth = exchange(NQ, lambda s: held.at[q], lambda s: held.at[q], sd, rd, in_z)
    for copy in fourth:
        copy.wait_recv()
    for k in range(3):
        o2_ref[k] = held[2 * k : 2 * k + 2].reshape(256, 128).astype(jnp.float32) * (131072.0 ** -0.5)
        piece = held[6 + k // 2, (k % 2) * 64 : (k % 2) * 64 + 64, :]
        o1_ref[k] = piece.astype(jnp.float32).T * (262144.0 ** -0.5)
    for copy in first + second + third + fourth:
        copy.wait_send()


def sum_over_frames(p1, p2):
    vmem = pl.BlockSpec(memory_space=pltpu.VMEM)
    dma = pltpu.SemaphoreType.DMA
    return pl.pallas_call(
        sum_kernel,
        out_shape=(
            jax.ShapeDtypeStruct((3, 128, 64), jnp.float32),
            jax.ShapeDtypeStruct((3, 256, 128), jnp.float32),
        ),
        in_specs=[vmem] * 2,
        out_specs=(vmem, vmem),
        scratch_shapes=[
            pltpu.VMEM((NQ, 128, 128), jnp.float32),
            pltpu.VMEM((NQ, 128, 128), jnp.bfloat16),
            pltpu.VMEM((NQ, 128, 128), jnp.bfloat16),
            pltpu.VMEM((NZ, 8, 128), jnp.float32),
            pltpu.VMEM((NZ, 8, 128), jnp.float32),
            pltpu.VMEM((NZ, 8, 128), jnp.float32),
            pltpu.VMEM((NQ, 128, 128), jnp.bfloat16),
            dma((NQ,)), dma((NQ,)), dma((NZ,)), dma((NZ,)),
            dma((NZ,)), dma((NZ,)), dma((NQ,)), dma((NQ,)),
        ],
        compiler_params=pltpu.CompilerParams(
            collective_id=0, has_side_effects=True, vmem_limit_bytes=24 * 1024 * 1024
        ),
    )(p1, p2)


def per_device(video, clip_start, first_conv_weight, second_conv_weight, cotangent):
    frames = video.shape[0]
    halved = frames // 2
    positions = video.shape[2]
    my_index = lax.axis_index("tm")
    tap_offsets = jnp.arange(3, dtype=jnp.int32)
    frame_global = my_index * frames + jnp.arange(frames, dtype=jnp.int32)
    first_source = (
        jnp.maximum(frame_global[:, None] - tap_offsets[None, :], clip_start[:, None])
        - my_index * frames
        + 2
    )
    full_input = lax.all_gather(video, "chan", axis=1, tiled=True)
    earlier_input = passed_along(full_input[frames - 2 :], "tm", 1)
    input_ext = jnp.concatenate([earlier_input, full_input], axis=0)
    pre_activation = jnp.zeros((frames, first_conv_weight.shape[2], positions), jnp.float32)
    for filter_tap in range(3):
        selected_frames = jnp.take(input_ext, first_source[:, filter_tap], axis=0)
        pre_activation = pre_activation + jnp.einsum(
            "em,reu->rmu",
            first_conv_weight[filter_tap],
            selected_frames,
            preferred_element_type=jnp.float32,
        )
    sigmoid_pre = jax.nn.sigmoid(pre_activation)
    activated = pre_activation * sigmoid_pre
    downsampled = (0.5 * (activated[0::2] + activated[1::2])).astype(jnp.bfloat16)
    half_global = my_index * halved + jnp.arange(halved, dtype=jnp.int32)
    start_two = clip_start[0::2] // 2
    second_source = (
        jnp.maximum(half_global[:, None] - tap_offsets[None, :], start_two[:, None])
        - my_index * halved
        + 2
    )
    full_middle = lax.all_gather(downsampled, "chan", axis=1, tiled=True)
    earlier_middle = passed_along(full_middle, "tm", 1)
    middle_ext = jnp.concatenate([earlier_middle, full_middle], axis=0)
    encoded = jnp.zeros((halved, second_conv_weight.shape[2], positions), jnp.float32)
    for filter_tap in range(3):
        selected_frames = jnp.take(middle_ext, second_source[:, filter_tap], axis=0)
        encoded = encoded + jnp.einsum(
            "em,reu->rmu",
            second_conv_weight[filter_tap],
            selected_frames,
            preferred_element_type=jnp.float32,
        )
    encoded = encoded.astype(jnp.bfloat16)
    target_rows = jnp.arange(halved + 2, dtype=jnp.int32)
    gathered_terms = jnp.zeros((halved + 2, second_conv_weight.shape[1], positions), jnp.float32)
    for filter_tap in range(3):
        tap_contribution = jnp.einsum(
            "jk,dkp->djp",
            second_conv_weight[filter_tap],
            cotangent,
            preferred_element_type=jnp.float32,
        )
        selector = (target_rows[:, None] == second_source[:, filter_tap][None, :]).astype(
            jnp.float32
        )
        gathered_terms = gathered_terms + jnp.einsum(
            "ij,jcs->ics", selector, tap_contribution, precision=lax.Precision.HIGHEST
        )
    spilled = passed_along(gathered_terms[:2], "tm", -1)
    local_terms = gathered_terms[2:].at[halved - 2 :].add(spilled)
    unit_grads = lax.psum_scatter(local_terms, "chan", scatter_dimension=1, tiled=True)
    delta = (
        0.5
        * jnp.repeat(unit_grads, 2, axis=0)
        * sigmoid_pre
        * (1.0 + pre_activation * (1.0 - sigmoid_pre))
    ).astype(jnp.bfloat16)
    first_weight_gradient = (
        jnp.stack(
            [
                jnp.einsum(
                    "rdm,rym->yd",
                    jnp.take(input_ext, first_source[:, filter_tap], axis=0),
                    delta,
                    preferred_element_type=jnp.float32,
                )
                for filter_tap in range(3)
            ]
        )
    )
    second_weight_gradient = (
        jnp.stack(
            [
                jnp.einsum(
                    "rdm,rym->dy",
                    jnp.take(middle_ext, second_source[:, filter_tap], axis=0),
                    cotangent,
                    preferred_element_type=jnp.float32,
                )
                for filter_tap in range(3)
            ]
        )
    )
    first_weight_gradient, second_weight_gradient = sum_over_frames(
        first_weight_gradient.reshape(192, 128), second_weight_gradient.reshape(768, 128)
    )
    return (encoded, first_weight_gradient, second_weight_gradient)


def solution(mesh):
    in_specs = (
        P("tm", "chan", None),
        P("tm"),
        P(None, None, "chan"),
        P(None, None, "chan"),
        P("tm", "chan", None),
    )
    out_specs = (P("tm", "chan", None), P(None, None, "chan"), P(None, None, "chan"))
    return jax.shard_map(
        per_device, mesh=mesh, in_specs=in_specs, out_specs=out_specs, check_vma=False
    )
```

```python
import jax
import jax.numpy as jnp
from jax import lax
from jax.experimental import pallas as pl
from jax.experimental.pallas import tpu as pltpu
from jax.sharding import PartitionSpec as P

MESH = pl.DeviceIdType.MESH
F32 = jnp.float32
BF16 = jnp.bfloat16
NQ = 8
NZ = 16
NX = 4
NT = NQ * NZ


def nt(a, b):
    return lax.dot_general(a, b, (((1,), (1,)), ((), ())), preferred_element_type=F32)


def nn(a, b):
    return lax.dot_general(a, b, (((1,), (0,)), ((), ())), preferred_element_type=F32)


def tn(a, b):
    return lax.dot_general(a, b, (((0,), (0,)), ((), ())), preferred_element_type=F32)


def kernel(
    clip_ref, video_ref, w1_ref, w2_ref, cot_ref,
    enc_ref, o1_ref, o2_ref,
    vext, coth, flags, flagh, uown, usend, urecv, pre, dsext,
    masks, part, send1, recv1, mine, recv2, gather, held,
    sva, rva, svb, rvb, svh, rvh, sct, rct, sfl, rfl, su, ru, sds, rds, sdh, rdh,
    sa, ra, sb, rb, sc, rc, sd, rd,
):
    me = lax.axis_index("tm")
    chan = lax.axis_index("chan")
    z, q = me // NQ, lax.rem(me, NQ)
    prev = (lax.rem(me + NT - 1, NT), chan)
    nxt = (lax.rem(me + 1, NT), chan)

    def in_z(s):
        return (z * NQ + lax.rem(q + s, NQ), chan)

    def over_z(s):
        return (lax.rem(z + s, NZ) * NQ + q, chan)

    def over_x(s):
        return (me, lax.rem(chan + s, NX))

    def signal(device):
        pl.semaphore_signal(barrier, inc=1, device_id=device, device_id_type=MESH)

    started = []

    def send(src, dst, ssem, rsem, device):
        copy = pltpu.make_async_remote_copy(
            src_ref=src, dst_ref=dst, send_sem=ssem, recv_sem=rsem,
            device_id=device, device_id_type=MESH,
        )
        copy.start()
        started.append(copy)
        return copy

    barrier = pltpu.get_barrier_semaphore()
    for s in range(1, NX):
        signal(over_x(s))
    signal(prev)
    signal(nxt)
    for s in range(1, NQ):
        signal(in_z(s))
    for s in range(1, NZ):
        signal(over_z(s))

    start = [clip_ref[t] - 4 * me for t in range(4)]
    start2 = [lax.shift_right_arithmetic(clip_ref[2 * j], 1) - 2 * me for j in range(2)]

    def flag(condition):
        return jnp.where(condition, 1.0, 0.0).astype(F32)

    rows = [start2[0] <= -1, start2[0] == -1, start2[0] <= -2, start2[1] <= -1]
    flags[...] = jnp.concatenate(
        [jnp.full((1, 512), flag(r), F32) for r in rows] + [jnp.zeros((12, 512), F32)], axis=0
    ).astype(BF16)

    def block(c, size):
        return pl.ds(pl.multiple_of(c * size, size), size)

    pl.semaphore_wait(barrier, (NX - 1) + 2 + (NQ - 1) + (NZ - 1))

    own = block(chan, 32)
    ahead = [None]
    for s in range(1, NX):
        ahead.append(send(video_ref.at[2:4], vext.at[4:6, own], sva.at[s], rva.at[s], over_x(s)))
    cot_copy = send(cot_ref, coth, sct, rct, prev)
    flag_copy = send(flags, flagh, sfl, rfl, prev)
    halo = [send(video_ref.at[2:4], vext.at[0:2, own], svh.at[0], rvh.at[0], nxt)]
    behind = [None]
    for s in range(1, NX):
        behind.append(send(video_ref.at[0:2], vext.at[2:4, own], svb.at[s], rvb.at[s], over_x(s)))
    vext[2:6, own, :] = video_ref[...]
    for s in range(1, NX):
        ahead[s].wait_recv()
        from_s = block(lax.rem(chan + NX - s, NX), 32)
        halo.append(send(vext.at[4:6, from_s], vext.at[0:2, from_s], svh.at[s], rvh.at[s], nxt))

    cot = [cot_ref[0], cot_ref[1]]

    def masked(x, condition):
        return x * flag(condition).astype(BF16)

    masks[0] = masked(cot[0], start2[0] == 0)
    masks[1] = masked(cot[1], start2[1] == 1)
    masks[2] = masked(cot[1], start2[1] <= 0)
    masks[3] = masked(cot[1], start2[1] == 0)
    a, b, c, d = (masks[i] for i in range(4))
    w2 = [w2_ref[k] for k in range(3)]
    local0 = nn(
        jnp.concatenate([w2[0], w2[1], w2[1], w2[2], w2[2]], axis=1),
        jnp.concatenate([cot[0], a, c, a, d], axis=0),
    )
    local1 = nn(
        jnp.concatenate([w2[0], w2[1], w2[2]], axis=1), jnp.concatenate([cot[1], b, b], axis=0)
    )
    cot_copy.wait_recv()
    flag_copy.wait_recv()
    later = [coth[0], coth[1]]
    for i in range(4):
        masks[4 + i] = later[i // 3] * flagh[i : i + 1, :]
    e, f, g, h = (masks[4 + i] for i in range(4))
    units = [
        local0 + nn(w2[2], g),
        local1 + nn(jnp.concatenate([w2[1], w2[2], w2[2]], axis=1), jnp.concatenate([e, f, h], axis=0)),
    ]
    for i in range(2):
        for x in range(NX):
            piece = units[i][64 * x : 64 * x + 64]
            uown[x, i] = piece
            usend[x, i] = piece.astype(BF16)
    sums = [None]
    for s in range(1, NX):
        sums.append(send(usend.at[lax.rem(chan + s, NX)], urecv.at[s], su.at[s], ru.at[s], over_x(s)))

    for s in range(1, NX):
        behind[s].wait_recv()
    for s in range(NX):
        halo[s].wait_recv()
    w1 = jnp.concatenate([w1_ref[k] for k in range(3)], axis=0)
    source = [[jnp.maximum(t - k, start[t]) + 2 for k in range(3)] for t in range(4)]
    mine64 = block(chan, 64)
    for j in range(2):
        total = None
        for t in (2 * j, 2 * j + 1):
            p = tn(w1, jnp.concatenate([vext[source[t][k]] for k in range(3)], axis=0))
            pre[t] = p
            act = p * jax.nn.sigmoid(p)
            total = act if total is None else total + act
        dsext[2 + j, mine64, :] = (0.5 * total).astype(BF16)
    spread = [None]
    for s in range(1, NX):
        spread.append(
            send(dsext.at[2:4, mine64], dsext.at[2:4, mine64], sds.at[s], rds.at[s], over_x(s))
        )
    dhalo = [send(dsext.at[2:4, mine64], dsext.at[0:2, mine64], sdh.at[0], rdh.at[0], nxt)]

    unit = uown[chan]
    for s in range(1, NX):
        sums[s].wait_recv()
        unit = unit + urecv[s].astype(F32)
    deltas = []
    for t in range(4):
        p = pre[t]
        sig = jax.nn.sigmoid(p)
        deltas.append((0.5 * unit[t // 2] * sig * (1.0 + p * (1.0 - sig))).astype(BF16))
    delta = jnp.concatenate(deltas, axis=1)
    for k in range(3):
        grad = nt(delta, jnp.concatenate([vext[source[t][k]] for t in range(4)], axis=1))
        part[6 + k // 2, 64 * (k % 2) : 64 * (k % 2) + 64, :] = grad
    part[7, 64:128, :] = jnp.zeros((64, 128), F32)

    for s in range(1, NX):
        spread[s].wait_recv()
        from_s = block(lax.rem(chan + NX - s, NX), 64)
        dhalo.append(send(dsext.at[2:4, from_s], dsext.at[0:2, from_s], sdh.at[s], rdh.at[s], nxt))
    cot = [cot_ref.at[0], cot_ref.at[1]]
    a, b, c, d, e, f, g, h = (masks.at[i] for i in range(8))
    terms = [
        [(0, cot[0]), (1, cot[1])],
        [(0, a), (1, b), (0, c), (1, e)],
        [(0, a), (1, b), (0, d), (1, f), (0, g), (1, h)],
    ]
    @pl.loop(0, 2)
    def _(half):
        for k in range(3):
            right = jnp.concatenate([v[...] for _, v in terms[k]], axis=1)
            left = [dsext[2 + i, block(half, 128), :] for i, _ in terms[k]]
            part[2 * k + half] = nt(jnp.concatenate(left, axis=1), right)

    send1[...] = part[...].astype(BF16)

    first = [None]
    for s in range(1, NQ):
        first.append(send(send1.at[lax.rem(q + s, NQ)], recv1.at[s], sa.at[s], ra.at[s], in_z(s)))

    for s in range(NX):
        dhalo[s].wait_recv()
    w2t = jnp.concatenate(w2, axis=0)
    for j in range(2):
        sources = [dsext[jnp.maximum(j - k, start2[j]) + 2] for k in range(3)]
        enc_ref[j] = tn(w2t, jnp.concatenate(sources, axis=0)).astype(BF16)

    total = part[q]
    for s in range(1, NQ):
        first[s].wait_recv()
        total = total + recv1[s].astype(F32)
    mine[...] = total.reshape(NZ, 8, 128)
    second = [None]
    for s in range(1, NZ):
        second.append(send(mine.at[lax.rem(z + s, NZ)], recv2.at[s], sb.at[s], rb.at[s], over_z(s)))
    total = mine[z]
    for s in range(1, NZ):
        second[s].wait_recv()
        total = total + recv2[s]
    gather[z] = total
    third = [send(gather.at[z], gather.at[z], sc.at[s], rc.at[s], over_z(s)) for s in range(1, NZ)]
    for copy in third:
        copy.wait_recv()
    held[q] = gather[...].reshape(128, 128).astype(BF16)
    fourth = [send(held.at[q], held.at[q], sd.at[s], rd.at[s], in_z(s)) for s in range(1, NQ)]
    for copy in fourth:
        copy.wait_recv()
    for k in range(3):
        o2_ref[k] = held[2 * k : 2 * k + 2].reshape(256, 128).astype(F32) * (131072.0 ** -0.5)
        piece = held[6 + k // 2, (k % 2) * 64 : (k % 2) * 64 + 64, :]
        o1_ref[k] = piece.astype(F32).T * (262144.0 ** -0.5)
    for copy in started:
        copy.wait_send()


def per_device(video, clip_start, first_conv_weight, second_conv_weight, cotangent):
    vmem = pl.BlockSpec(memory_space=pltpu.VMEM)
    smem = pl.BlockSpec(memory_space=pltpu.SMEM)
    dma = pltpu.SemaphoreType.DMA
    return pl.pallas_call(
        kernel,
        out_shape=(
            jax.ShapeDtypeStruct((2, 128, 512), BF16),
            jax.ShapeDtypeStruct((3, 128, 64), F32),
            jax.ShapeDtypeStruct((3, 256, 128), F32),
        ),
        in_specs=[smem, vmem, vmem, vmem, vmem],
        out_specs=(vmem, vmem, vmem),
        scratch_shapes=[
            pltpu.VMEM((6, 128, 512), BF16),
            pltpu.VMEM((2, 128, 512), BF16),
            pltpu.VMEM((16, 512), BF16),
            pltpu.VMEM((16, 512), BF16),
            pltpu.VMEM((NX, 2, 64, 512), F32),
            pltpu.VMEM((NX, 2, 64, 512), BF16),
            pltpu.VMEM((NX, 2, 64, 512), BF16),
            pltpu.VMEM((4, 64, 512), F32),
            pltpu.VMEM((4, 256, 512), BF16),
            pltpu.VMEM((8, 128, 512), BF16),
            pltpu.VMEM((NQ, 128, 128), F32),
            pltpu.VMEM((NQ, 128, 128), BF16),
            pltpu.VMEM((NQ, 128, 128), BF16),
            pltpu.VMEM((NZ, 8, 128), F32),
            pltpu.VMEM((NZ, 8, 128), F32),
            pltpu.VMEM((NZ, 8, 128), F32),
            pltpu.VMEM((NQ, 128, 128), BF16),
        ]
        + [dma((NX,))] * 6
        + [dma(())] * 4
        + [dma((NX,))] * 6
        + [dma((NQ,)), dma((NQ,)), dma((NZ,)), dma((NZ,)), dma((NZ,)), dma((NZ,)), dma((NQ,)), dma((NQ,))],
        compiler_params=pltpu.CompilerParams(
            collective_id=0, has_side_effects=True, vmem_limit_bytes=40 * 1024 * 1024
        ),
    )(clip_start, video, first_conv_weight, second_conv_weight, cotangent)


def solution(mesh):
    in_specs = (
        P("tm", "chan", None),
        P("tm"),
        P(None, None, "chan"),
        P(None, None, "chan"),
        P("tm", "chan", None),
    )
    out_specs = (P("tm", "chan", None), P(None, None, "chan"), P(None, None, "chan"))
    return jax.shard_map(
        per_device, mesh=mesh, in_specs=in_specs, out_specs=out_specs, check_vma=False
    )
```

```python
import jax
import jax.numpy as jnp
from jax import lax
from jax.experimental import pallas as pl
from jax.experimental.pallas import tpu as pltpu
from jax.sharding import PartitionSpec as P

MESH = pl.DeviceIdType.MESH
F32 = jnp.float32
BF16 = jnp.bfloat16
NQ = 8
NZ = 16
NX = 4
NT = NQ * NZ


def nt(a, b):
    return lax.dot_general(a, b, (((1,), (1,)), ((), ())), preferred_element_type=F32)


def nn(a, b):
    return lax.dot_general(a, b, (((1,), (0,)), ((), ())), preferred_element_type=F32)


def tn(a, b):
    return lax.dot_general(a, b, (((0,), (0,)), ((), ())), preferred_element_type=F32)


def kernel(
    clip_hbm, video_hbm, w1_hbm, w2_hbm, cot_hbm,
    enc_ref, held,
    clip_ref, w1_ref, w2_ref, cot_ref,
    vown, vhalo, coth, flags, flagh, uown, usend, urecv, pre, dsext,
    masks, part, send1, recv1, tiles, recv2, final,
    sin, sva, rva, svb, rvb, svh, rvh, sct, rct, sfl, rfl, su, ru, sds, rds, sdh, rdh,
    sa, ra, sb, rb, sc, rc, sd, rd, known,
):
    me = lax.axis_index("tm")
    chan = lax.axis_index("chan")
    z, q = me // NQ, lax.rem(me, NQ)
    prev = (lax.rem(me + NT - 1, NT), chan)
    nxt = (lax.rem(me + 1, NT), chan)

    def in_z(s):
        return (z * NQ + lax.rem(q + s, NQ), chan)

    def over_z(s):
        return (lax.rem(z + s, NZ) * NQ + q, chan)

    def over_x(s):
        return (me, lax.rem(chan + s, NX))

    def block(c, size):
        return pl.ds(pl.multiple_of(c * size, size), size)

    def remote(src, dst, ssem, rsem, device):
        return pltpu.make_async_remote_copy(
            src_ref=src, dst_ref=dst, send_sem=ssem, recv_sem=rsem,
            device_id=device, device_id_type=MESH,
        )

    started = []

    def send(src, dst, ssem, rsem, device):
        copy = remote(src, dst, ssem, rsem, device)
        copy.start()
        started.append(copy)
        return copy

    barrier = pltpu.get_barrier_semaphore()
    near = [over_x(s) for s in range(1, NX)] + [prev, nxt, over_z(1), over_z(NZ - 1)]
    near += [in_z(s) for s in range(1, NQ)]
    for device in near:
        pl.semaphore_signal(barrier, inc=1, device_id=device, device_id_type=MESH)

    own = block(chan, 32)
    fetch = [
        pltpu.make_async_copy(src, dst, sin.at[i])
        for i, (src, dst) in enumerate([
            (clip_hbm, clip_ref), (cot_hbm, cot_ref), (w2_hbm, w2_ref), (w1_hbm, w1_ref),
            (video_hbm, vown.at[:, own]),
        ])
    ]
    for copy in fetch:
        copy.start()
    fetch[0].wait()

    start = [clip_ref[t] - 4 * me for t in range(4)]
    start2 = [lax.shift_right_arithmetic(clip_ref[2 * j], 1) - 2 * me for j in range(2)]

    def flag(condition):
        return jnp.where(condition, 1.0, 0.0).astype(F32)

    rows = [start2[0] <= -1, start2[0] == -1, start2[0] <= -2, start2[1] <= -1]
    flags[...] = jnp.concatenate(
        [jnp.full((1, 512), flag(r), F32) for r in rows] + [jnp.zeros((12, 512), F32)], axis=0
    ).astype(BF16)

    pl.semaphore_wait(barrier, len(near))

    ahead, behind, halo = [None], [None], []
    for s in range(1, NX):
        ahead.append(send(video_hbm.at[2:4], vown.at[2:4, own], sva.at[s], rva.at[s], over_x(s)))
    halo.append(send(video_hbm.at[2:4], vhalo.at[:, own], svh.at[0], rvh.at[0], nxt))
    for s in range(1, NX):
        behind.append(send(video_hbm.at[0:2], vown.at[0:2, own], svb.at[s], rvb.at[s], over_x(s)))
    cot_copy = send(cot_hbm, coth, sct, rct, prev)
    flag_copy = send(flags, flagh, sfl, rfl, prev)

    def greet(step, distance):
        for s in (distance, NZ - distance):
            pl.semaphore_signal(known.at[step], inc=1, device_id=over_z(s), device_id_type=MESH)

    greet(0, 1)

    for copy in fetch[1:]:
        copy.wait()

    def masked(x, condition):
        return x * flag(condition).astype(BF16)

    cot = [cot_ref[0], cot_ref[1]]
    masks[0] = masked(cot[0], start2[0] == 0)
    masks[1] = masked(cot[1], start2[1] == 1)
    masks[2] = masked(cot[1], start2[1] <= 0)
    masks[3] = masked(cot[1], start2[1] == 0)
    a, b, c, d = (masks[i] for i in range(4))
    w2 = [w2_ref[k] for k in range(3)]
    local0 = nn(
        jnp.concatenate([w2[0], w2[1], w2[1], w2[2], w2[2]], axis=1),
        jnp.concatenate([cot[0], a, c, a, d], axis=0),
    )
    local1 = nn(
        jnp.concatenate([w2[0], w2[1], w2[2]], axis=1), jnp.concatenate([cot[1], b, b], axis=0)
    )
    cot_copy.wait_recv()
    flag_copy.wait_recv()
    for i in range(4):
        masks[4 + i] = coth[i // 3] * flagh[i : i + 1, :]
    e, f, g, h = (masks[4 + i] for i in range(4))
    units = [
        local0 + nn(w2[2], g),
        local1 + nn(jnp.concatenate([w2[1], w2[2], w2[2]], axis=1), jnp.concatenate([e, f, h], axis=0)),
    ]
    for i in range(2):
        for x in range(NX):
            piece = units[i][64 * x : 64 * x + 64]
            uown[x, i] = piece
            usend[x, i] = piece.astype(BF16)

    pl.semaphore_wait(known.at[0], 2)
    greet(1, 2)

    for s in range(1, NX):
        ahead[s].wait_recv()
        from_s = block(lax.rem(chan + NX - s, NX), 32)
        halo.append(send(vown.at[2:4, from_s], vhalo.at[:, from_s], svh.at[s], rvh.at[s], nxt))
    for s in range(1, NX):
        behind[s].wait_recv()
    sums = [None]
    for s in range(1, NX):
        sums.append(send(usend.at[lax.rem(chan + s, NX)], urecv.at[s], su.at[s], ru.at[s], over_x(s)))
    pl.semaphore_wait(known.at[1], 2)
    greet(2, 4)

    w1 = jnp.concatenate([w1_ref[k] for k in range(3)], axis=1)
    mine64 = block(chan, 64)

    def source(t, k):
        if k == 0:
            return vown[t]
        index = jnp.maximum(t - k, start[t])
        inside = vown[jnp.maximum(index, 0)]
        if t >= k:
            return inside
        return jnp.where(index < 0, vhalo[jnp.clip(index + 2, 0, 1)], inside)

    spread, dhalo = {}, {}
    for j in (1, 0):
        if j == 0:
            for s in range(NX):
                halo[s].wait_recv()
        total = None
        for t in (2 * j, 2 * j + 1):
            p = nn(w1, jnp.concatenate([source(t, k) for k in range(3)], axis=0))
            pre[t] = p
            act = p * jax.nn.sigmoid(p)
            total = act if total is None else total + act
        dsext[2 + j, mine64, :] = (0.5 * total).astype(BF16)
        row = dsext.at[2 + j, mine64]
        for s in range(1, NX):
            spread[j, s] = send(row, row, sds.at[j, s], rds.at[j, s], over_x(s))
    dhalo[0] = send(dsext.at[2:4, mine64], dsext.at[0:2, mine64], sdh.at[0], rdh.at[0], nxt)

    def hand_over(piece):
        send1[piece] = part[piece].astype(BF16)
        s = lax.rem(piece + NQ - q, NQ)

        @pl.when(s != 0)
        def _():
            remote(send1.at[piece], recv1.at[s], sa.at[piece], ra.at[s], (z * NQ + piece, chan)).start()

    unit = uown[chan]
    for s in range(1, NX):
        sums[s].wait_recv()
        unit = unit + urecv[s].astype(F32)
    deltas = []
    for t in range(4):
        p = pre[t]
        sig = jax.nn.sigmoid(p)
        deltas.append((0.5 * unit[t // 2] * sig * (1.0 + p * (1.0 - sig))).astype(BF16))
    delta = jnp.concatenate(deltas, axis=1)
    for k in range(3):
        grad = nt(delta, jnp.concatenate([source(t, k) for t in range(4)], axis=1))
        part[6 + k // 2, 64 * (k % 2) : 64 * (k % 2) + 64, :] = grad
    part[7, 64:128, :] = jnp.zeros((64, 128), F32)
    hand_over(6)
    hand_over(7)
    pl.semaphore_wait(known.at[2], 2)

    for s in range(1, NX):
        from_s = block(lax.rem(chan + NX - s, NX), 64)
        for j in (1, 0):
            spread[j, s].wait_recv()
        dhalo[s] = send(dsext.at[2:4, from_s], dsext.at[0:2, from_s], sdh.at[s], rdh.at[s], nxt)
    cot = [cot_ref.at[0], cot_ref.at[1]]
    a, b, c, d, e, f, g, h = (masks.at[i] for i in range(8))
    terms = [
        [(0, cot[0]), (1, cot[1])],
        [(0, a), (1, b), (0, c), (1, e)],
        [(0, a), (1, b), (0, d), (1, f), (0, g), (1, h)],
    ]

    @pl.loop(0, 2)
    def _(half):
        for k in range(3):
            right = jnp.concatenate([v[...] for _, v in terms[k]], axis=1)
            left = [dsext[2 + i, block(half, 128), :] for i, _ in terms[k]]
            part[2 * k + half] = nt(jnp.concatenate(left, axis=1), right)
            hand_over(2 * k + half)

    for s in range(NX):
        dhalo[s].wait_recv()
    w2t = jnp.concatenate([w2_ref[k] for k in range(3)], axis=0)
    for j in range(2):
        sources = [dsext[jnp.maximum(j - k, start2[j]) + 2] for k in range(3)]
        enc_ref[j] = tn(w2t, jnp.concatenate(sources, axis=0)).astype(BF16)

    total = part[q]
    for s in range(1, NQ):
        remote(send1.at[0], recv1.at[s], sa.at[0], ra.at[s], in_z(s)).wait_recv()
        total = total + recv1[s].astype(F32)
    tiles[...] = total.astype(BF16).reshape(8, 16, 128)

    owner = lax.rem(z + q, 2) == 0
    mine = z // 2

    def tile_of(s):
        return lax.rem(z + s, NZ) // 2

    @pl.when(owner)
    def _():
        first = [
            remote(tiles.at[tile_of(s)], recv2.at[s], sb.at[s], rb.at[s], over_z(s))
            for s in range(1, NZ)
        ]
        for s in range(2, NZ, 2):
            first[s - 1].start()
        total = tiles[mine].astype(F32)
        for s in range(1, NZ):
            first[s - 1].wait_recv()
            total = total + recv2[s].astype(F32)
        final[mine] = total.astype(BF16)
        second = [
            remote(final.at[mine], final.at[mine], sc.at[s], rc.at[s], over_z(s))
            for s in range(1, NZ)
        ]
        for copy in second:
            copy.start()
        for s in range(2, NZ, 2):
            second[s - 1].wait_recv()
            first[s - 1].wait_send()
        for copy in second:
            copy.wait_send()

    @pl.when(jnp.logical_not(owner))
    def _():
        first = [
            remote(tiles.at[tile_of(s)], recv2.at[s], sb.at[s], rb.at[s], over_z(s))
            for s in range(1, NZ, 2)
        ]
        for copy in first:
            copy.start()
        for s in range(1, NZ, 2):
            remote(final.at[mine], final.at[mine], sc.at[s], rc.at[s], over_z(s)).wait_recv()
        for copy in first:
            copy.wait_send()

    held[q] = final[...].reshape(128, 128)
    fourth = [send(held.at[q], held.at[q], sd.at[s], rd.at[s], in_z(s)) for s in range(1, NQ)]
    for piece in range(NQ):
        @pl.when(piece != q)
        def _():
            remote(send1.at[piece], recv1.at[1], sa.at[piece], ra.at[1], nxt).wait_send()
    for copy in fourth:
        copy.wait_recv()
    for copy in started:
        copy.wait_send()


def write_kernel(enc_ref, held, out_ref, o1_ref, o2_ref):
    out_ref[...] = enc_ref[...]
    for k in range(3):
        o2_ref[k] = held[2 * k : 2 * k + 2].reshape(256, 128).astype(F32) * (131072.0 ** -0.5)
        piece = held[6 + k // 2, (k % 2) * 64 : (k % 2) * 64 + 64, :]
        o1_ref[k] = piece.astype(F32) * (262144.0 ** -0.5)


def per_device(video, clip_start, first_conv_weight, second_conv_weight, cotangent):
    vmem = pl.BlockSpec(memory_space=pltpu.VMEM)
    hbm = pl.BlockSpec(memory_space=pltpu.HBM)
    dma = pltpu.SemaphoreType.DMA
    encoded, held = pl.pallas_call(
        kernel,
        out_shape=(
            jax.ShapeDtypeStruct((2, 128, 512), BF16),
            jax.ShapeDtypeStruct((NQ, 128, 128), BF16),
        ),
        in_specs=[hbm] * 5,
        out_specs=(vmem, vmem),
        scratch_shapes=[
            pltpu.SMEM((4,), jnp.int32),
            pltpu.VMEM((3, 64, 128), BF16),
            pltpu.VMEM((3, 256, 128), BF16),
            pltpu.VMEM((2, 128, 512), BF16),
            pltpu.VMEM((4, 128, 512), BF16),
            pltpu.VMEM((2, 128, 512), BF16),
            pltpu.VMEM((2, 128, 512), BF16),
            pltpu.VMEM((16, 512), BF16),
            pltpu.VMEM((16, 512), BF16),
            pltpu.VMEM((NX, 2, 64, 512), F32),
            pltpu.VMEM((NX, 2, 64, 512), BF16),
            pltpu.VMEM((NX, 2, 64, 512), BF16),
            pltpu.VMEM((4, 64, 512), F32),
            pltpu.VMEM((4, 256, 512), BF16),
            pltpu.VMEM((8, 128, 512), BF16),
            pltpu.VMEM((NQ, 128, 128), F32),
            pltpu.VMEM((NQ, 128, 128), BF16),
            pltpu.VMEM((NQ, 128, 128), BF16),
            pltpu.VMEM((8, 16, 128), BF16),
            pltpu.VMEM((NZ, 16, 128), BF16),
            pltpu.VMEM((8, 16, 128), BF16),
            dma((5,)),
        ]
        + [dma((NX,))] * 6
        + [dma(())] * 4
        + [dma((NX,))] * 2
        + [dma((2, NX))] * 2
        + [dma((NX,))] * 2
        + [dma((NQ,)), dma((NQ,)), dma((NZ,)), dma((NZ,)), dma((NZ,)), dma((NZ,)), dma((NQ,)), dma((NQ,))]
        + [pltpu.SemaphoreType.REGULAR((3,))],
        compiler_params=pltpu.CompilerParams(
            collective_id=0, has_side_effects=True, vmem_limit_bytes=62 * 1024 * 1024
        ),
    )(clip_start, video, first_conv_weight.transpose(0, 2, 1), second_conv_weight, cotangent)
    encoded, first_grad, second_grad = pl.pallas_call(
        write_kernel,
        out_shape=(
            jax.ShapeDtypeStruct((2, 128, 512), BF16),
            jax.ShapeDtypeStruct((3, 64, 128), F32),
            jax.ShapeDtypeStruct((3, 256, 128), F32),
        ),
        in_specs=[vmem] * 2,
        out_specs=(vmem,) * 3,
    )(encoded, held)
    return encoded, first_grad.transpose(0, 2, 1), second_grad


def solution(mesh):
    in_specs = (
        P("tm", "chan", None),
        P("tm"),
        P(None, None, "chan"),
        P(None, None, "chan"),
        P("tm", "chan", None),
    )
    out_specs = (P("tm", "chan", None), P(None, None, "chan"), P(None, None, "chan"))
    return jax.shard_map(
        per_device, mesh=mesh, in_specs=in_specs, out_specs=out_specs, check_vma=False
    )
```

```python
import jax
import jax.numpy as jnp
from jax import lax
from jax.experimental import pallas as pl
from jax.experimental.pallas import tpu as pltpu
from jax.sharding import PartitionSpec as P

MESH = pl.DeviceIdType.MESH
F32 = jnp.float32
BF16 = jnp.bfloat16
NQ = 8
NZ = 16
NX = 4
NT = NQ * NZ


def nt(a, b):
    return lax.dot_general(a, b, (((1,), (1,)), ((), ())), preferred_element_type=F32)


def nn(a, b):
    return lax.dot_general(a, b, (((1,), (0,)), ((), ())), preferred_element_type=F32)


def tn(a, b):
    return lax.dot_general(a, b, (((0,), (0,)), ((), ())), preferred_element_type=F32)


def kernel(
    clip_hbm, video_hbm, w1_hbm, w2_hbm, cot_hbm,
    enc_ref, held,
    clip_ref, w1_ref, w2_ref, cot_ref,
    vown, vhalo, coth, flags, flagh, uown, usend, urecv, pre, dsext,
    masks, part, send1, recv1, tiles, recv2, final,
    sin, sva, rva, svb, rvb, svh, rvh, sct, rct, sfl, rfl, su, ru, sw, rw, sdh, rdh,
    sa, ra, sb, rb, sc, rc, sd, rd, known,
):
    me = lax.axis_index("tm")
    chan = lax.axis_index("chan")
    z, q = me // NQ, lax.rem(me, NQ)
    prev = (lax.rem(me + NT - 1, NT), chan)
    nxt = (lax.rem(me + 1, NT), chan)

    def in_z(s):
        return (z * NQ + lax.rem(q + s, NQ), chan)

    def over_z(s):
        return (lax.rem(z + s, NZ) * NQ + q, chan)

    def over_x(s):
        return (me, lax.rem(chan + s, NX))

    def block(c, size):
        return pl.ds(pl.multiple_of(c * size, size), size)

    def remote(src, dst, ssem, rsem, device):
        return pltpu.make_async_remote_copy(
            src_ref=src, dst_ref=dst, send_sem=ssem, recv_sem=rsem,
            device_id=device, device_id_type=MESH,
        )

    started = []

    def send(src, dst, ssem, rsem, device):
        copy = remote(src, dst, ssem, rsem, device)
        copy.start()
        started.append(copy)
        return copy

    barrier = pltpu.get_barrier_semaphore()
    near = [over_x(s) for s in range(1, NX)] + [prev, nxt, over_z(1), over_z(NZ - 1)]
    near += [in_z(s) for s in range(1, NQ)]
    for device in near:
        pl.semaphore_signal(barrier, inc=1, device_id=device, device_id_type=MESH)

    own, mine64 = block(chan, 32), block(chan, 64)
    fetch = [
        pltpu.make_async_copy(src, dst, sin.at[i])
        for i, (src, dst) in enumerate([
            (clip_hbm, clip_ref), (cot_hbm, cot_ref), (w2_hbm, w2_ref), (w1_hbm, w1_ref.at[:, mine64]),
            (video_hbm, vown.at[:, own]),
        ])
    ]
    for copy in fetch:
        copy.start()
    fetch[0].wait()

    start = [clip_ref[t] - 4 * me for t in range(4)]
    start2 = [lax.shift_right_arithmetic(clip_ref[2 * j], 1) - 2 * me for j in range(2)]

    def flag(condition):
        return jnp.where(condition, 1.0, 0.0).astype(F32)

    rows = [start2[0] <= -1, start2[0] == -1, start2[0] <= -2, start2[1] <= -1]
    flags[...] = jnp.concatenate(
        [jnp.full((1, 512), flag(r), F32) for r in rows] + [jnp.zeros((12, 512), F32)], axis=0
    ).astype(BF16)

    pl.semaphore_wait(barrier, len(near))

    ahead, behind, halo = [None], [None], []
    for s in range(1, NX):
        ahead.append(send(video_hbm.at[2:4], vown.at[2:4, own], sva.at[s], rva.at[s], over_x(s)))
    halo.append(send(video_hbm.at[2:4], vhalo.at[:, own], svh.at[0], rvh.at[0], nxt))
    weights = [None]
    for s in range(1, NX):
        weights.append(send(w1_hbm, w1_ref.at[:, mine64], sw.at[s], rw.at[s], over_x(s)))
    for s in range(1, NX):
        behind.append(send(video_hbm.at[0:2], vown.at[0:2, own], svb.at[s], rvb.at[s], over_x(s)))
    cot_copy = send(cot_hbm, coth, sct, rct, prev)
    flag_copy = send(flags, flagh, sfl, rfl, prev)

    def greet(step, distance):
        for s in (distance, NZ - distance):
            pl.semaphore_signal(known.at[step], inc=1, device_id=over_z(s), device_id_type=MESH)

    greet(0, 1)

    for copy in fetch[1:]:
        copy.wait()

    def masked(x, condition):
        return x * flag(condition).astype(BF16)

    cot = [cot_ref[0], cot_ref[1]]
    masks[0] = masked(cot[0], start2[0] == 0)
    masks[1] = masked(cot[1], start2[1] == 1)
    masks[2] = masked(cot[1], start2[1] <= 0)
    masks[3] = masked(cot[1], start2[1] == 0)
    a, b, c, d = (masks[i] for i in range(4))
    w2 = [w2_ref[k] for k in range(3)]
    local0 = nn(
        jnp.concatenate([w2[0], w2[1], w2[1], w2[2], w2[2]], axis=1),
        jnp.concatenate([cot[0], a, c, a, d], axis=0),
    )
    local1 = nn(
        jnp.concatenate([w2[0], w2[1], w2[2]], axis=1), jnp.concatenate([cot[1], b, b], axis=0)
    )
    cot_copy.wait_recv()
    flag_copy.wait_recv()
    for i in range(4):
        masks[4 + i] = coth[i // 3] * flagh[i : i + 1, :]
    e, f, g, h = (masks[4 + i] for i in range(4))
    units = [
        local0 + nn(w2[2], g),
        local1 + nn(jnp.concatenate([w2[1], w2[2], w2[2]], axis=1), jnp.concatenate([e, f, h], axis=0)),
    ]
    for i in range(2):
        for x in range(NX):
            piece = units[i][64 * x : 64 * x + 64]
            uown[x, i] = piece
            usend[x, i] = piece.astype(BF16)

    pl.semaphore_wait(known.at[0], 2)
    greet(1, 2)

    for s in range(1, NX):
        ahead[s].wait_recv()
        from_s = block(lax.rem(chan + NX - s, NX), 32)
        halo.append(send(vown.at[2:4, from_s], vhalo.at[:, from_s], svh.at[s], rvh.at[s], nxt))
    for s in range(1, NX):
        behind[s].wait_recv()
    sums = [None]
    for s in range(1, NX):
        sums.append(send(usend.at[lax.rem(chan + s, NX)], urecv.at[s], su.at[s], ru.at[s], over_x(s)))
    pl.semaphore_wait(known.at[1], 2)
    greet(2, 4)

    for s in range(1, NX):
        weights[s].wait_recv()
    w1 = jnp.concatenate([w1_ref[k] for k in range(3)], axis=1)

    def source(t, k):
        if k == 0:
            return vown[t]
        index = jnp.maximum(t - k, start[t])
        inside = vown[jnp.maximum(index, 0)]
        if t >= k:
            return inside
        return jnp.where(index < 0, vhalo[jnp.clip(index + 2, 0, 1)], inside)

    for j in (1, 0):
        if j == 0:
            for s in range(NX):
                halo[s].wait_recv()
        total = None
        for t in (2 * j, 2 * j + 1):
            p = nn(w1, jnp.concatenate([source(t, k) for k in range(3)], axis=0))
            pre[t] = p
            act = p * jax.nn.sigmoid(p)
            total = act if total is None else total + act
        dsext[2 + j] = (0.5 * total).astype(BF16)

    def hand_over(piece):
        send1[piece] = part[piece].astype(BF16)
        s = lax.rem(piece + NQ - q, NQ)

        @pl.when(s != 0)
        def _():
            remote(send1.at[piece], recv1.at[s], sa.at[piece], ra.at[s], (z * NQ + piece, chan)).start()

    cot = [cot_ref.at[0], cot_ref.at[1]]
    a, b, c, d, e, f, g, h = (masks.at[i] for i in range(8))
    terms = [
        [(0, cot[0]), (1, cot[1])],
        [(0, a), (1, b), (0, c), (1, e)],
        [(0, a), (1, b), (0, d), (1, f), (0, g), (1, h)],
    ]

    @pl.loop(0, 2)
    def _(half):
        for k in range(3):
            right = jnp.concatenate([v[...] for _, v in terms[k]], axis=1)
            left = [dsext[2 + i, block(half, 128), :] for i, _ in terms[k]]
            part[2 * k + half] = nt(jnp.concatenate(left, axis=1), right)
            hand_over(2 * k + half)

    unit = uown[chan]
    for s in range(1, NX):
        sums[s].wait_recv()
        unit = unit + urecv[s].astype(F32)
    deltas = []
    for t in range(4):
        p = pre[t, mine64, :]
        sig = jax.nn.sigmoid(p)
        deltas.append((0.5 * unit[t // 2] * sig * (1.0 + p * (1.0 - sig))).astype(BF16))
    delta = jnp.concatenate(deltas, axis=1)
    for k in range(3):
        grad = nt(delta, jnp.concatenate([source(t, k) for t in range(4)], axis=1))
        part[6 + k // 2, 64 * (k % 2) : 64 * (k % 2) + 64, :] = grad
    part[7, 64:128, :] = jnp.zeros((64, 128), F32)
    hand_over(6)
    hand_over(7)
    dhalo = send(dsext.at[2:4], dsext.at[0:2], sdh, rdh, nxt)
    pl.semaphore_wait(known.at[2], 2)

    total = part[q]
    for s in range(1, NQ):
        remote(send1.at[0], recv1.at[s], sa.at[0], ra.at[s], in_z(s)).wait_recv()
        total = total + recv1[s].astype(F32)
    tiles[...] = total.astype(BF16).reshape(8, 16, 128)

    owner = lax.rem(z + q, 2) == 0
    mine = z // 2

    def tile_of(s):
        return lax.rem(z + s, NZ) // 2

    def to_owner(s):
        return remote(tiles.at[tile_of(s)], recv2.at[s], sb.at[s], rb.at[s], over_z(s))

    def from_owner(s):
        return remote(final.at[mine], final.at[mine], sc.at[s], rc.at[s], over_z(s))

    @pl.when(owner)
    def _():
        for s in range(2, NZ, 2):
            to_owner(s).start()

    @pl.when(jnp.logical_not(owner))
    def _():
        for s in range(1, NZ, 2):
            to_owner(s).start()

    dhalo.wait_recv()
    w2t = jnp.concatenate([w2_ref[k] for k in range(3)], axis=0)
    for j in range(2):
        sources = [dsext[jnp.maximum(j - k, start2[j]) + 2] for k in range(3)]
        enc_ref[j] = tn(w2t, jnp.concatenate(sources, axis=0)).astype(BF16)

    @pl.when(owner)
    def _():
        total = tiles[mine].astype(F32)
        for s in range(1, NZ):
            to_owner(s).wait_recv()
            total = total + recv2[s].astype(F32)
        final[mine] = total.astype(BF16)
        for s in range(1, NZ):
            from_owner(s).start()
        for s in range(2, NZ, 2):
            from_owner(s).wait_recv()
            to_owner(s).wait_send()
        for s in range(1, NZ):
            from_owner(s).wait_send()

    @pl.when(jnp.logical_not(owner))
    def _():
        for s in range(1, NZ, 2):
            from_owner(s).wait_recv()
            to_owner(s).wait_send()

    held[q] = final[...].reshape(128, 128)
    fourth = [send(held.at[q], held.at[q], sd.at[s], rd.at[s], in_z(s)) for s in range(1, NQ)]
    for piece in range(NQ):
        @pl.when(piece != q)
        def _():
            remote(send1.at[piece], recv1.at[1], sa.at[piece], ra.at[1], nxt).wait_send()
    for copy in fourth:
        copy.wait_recv()
    for copy in started:
        copy.wait_send()


def write_kernel(enc_ref, held, out_ref, o1_ref, o2_ref):
    out_ref[...] = enc_ref[...]
    for k in range(3):
        o2_ref[k] = held[2 * k : 2 * k + 2].reshape(256, 128).astype(F32) * (131072.0 ** -0.5)
        piece = held[6 + k // 2, (k % 2) * 64 : (k % 2) * 64 + 64, :]
        o1_ref[k] = piece.astype(F32) * (262144.0 ** -0.5)


def per_device(video, clip_start, first_conv_weight, second_conv_weight, cotangent):
    vmem = pl.BlockSpec(memory_space=pltpu.VMEM)
    hbm = pl.BlockSpec(memory_space=pltpu.HBM)
    dma = pltpu.SemaphoreType.DMA
    encoded, held = pl.pallas_call(
        kernel,
        out_shape=(
            jax.ShapeDtypeStruct((2, 128, 512), BF16),
            jax.ShapeDtypeStruct((NQ, 128, 128), BF16),
        ),
        in_specs=[hbm] * 5,
        out_specs=(vmem, vmem),
        scratch_shapes=[
            pltpu.SMEM((4,), jnp.int32),
            pltpu.VMEM((3, 256, 128), BF16),
            pltpu.VMEM((3, 256, 128), BF16),
            pltpu.VMEM((2, 128, 512), BF16),
            pltpu.VMEM((4, 128, 512), BF16),
            pltpu.VMEM((2, 128, 512), BF16),
            pltpu.VMEM((2, 128, 512), BF16),
            pltpu.VMEM((16, 512), BF16),
            pltpu.VMEM((16, 512), BF16),
            pltpu.VMEM((NX, 2, 64, 512), F32),
            pltpu.VMEM((NX, 2, 64, 512), BF16),
            pltpu.VMEM((NX, 2, 64, 512), BF16),
            pltpu.VMEM((4, 256, 512), F32),
            pltpu.VMEM((4, 256, 512), BF16),
            pltpu.VMEM((8, 128, 512), BF16),
            pltpu.VMEM((NQ, 128, 128), F32),
            pltpu.VMEM((NQ, 128, 128), BF16),
            pltpu.VMEM((NQ, 128, 128), BF16),
            pltpu.VMEM((8, 16, 128), BF16),
            pltpu.VMEM((NZ, 16, 128), BF16),
            pltpu.VMEM((8, 16, 128), BF16),
            dma((5,)),
        ]
        + [dma((NX,))] * 6
        + [dma(())] * 4
        + [dma((NX,))] * 4
        + [dma(())] * 2
        + [dma((NQ,)), dma((NQ,)), dma((NZ,)), dma((NZ,)), dma((NZ,)), dma((NZ,)), dma((NQ,)), dma((NQ,))]
        + [pltpu.SemaphoreType.REGULAR((3,))],
        compiler_params=pltpu.CompilerParams(
            collective_id=0, has_side_effects=True, vmem_limit_bytes=62 * 1024 * 1024
        ),
    )(clip_start, video, first_conv_weight.transpose(0, 2, 1), second_conv_weight, cotangent)
    encoded, first_grad, second_grad = pl.pallas_call(
        write_kernel,
        out_shape=(
            jax.ShapeDtypeStruct((2, 128, 512), BF16),
            jax.ShapeDtypeStruct((3, 64, 128), F32),
            jax.ShapeDtypeStruct((3, 256, 128), F32),
        ),
        in_specs=[vmem] * 2,
        out_specs=(vmem,) * 3,
    )(encoded, held)
    return encoded, first_grad.transpose(0, 2, 1), second_grad


def solution(mesh):
    in_specs = (
        P("tm", "chan", None),
        P("tm"),
        P(None, None, "chan"),
        P(None, None, "chan"),
        P("tm", "chan", None),
    )
    out_specs = (P("tm", "chan", None), P(None, None, "chan"), P(None, None, "chan"))
    return jax.shard_map(
        per_device, mesh=mesh, in_specs=in_specs, out_specs=out_specs, check_vma=False
    )
```

```python
import jax
import jax.numpy as jnp
from jax import lax
from jax.experimental import pallas as pl
from jax.experimental.pallas import tpu as pltpu
from jax.sharding import PartitionSpec as P

MESH = pl.DeviceIdType.MESH
F32 = jnp.float32
BF16 = jnp.bfloat16
NQ = 8
NZ = 16
NX = 4
NT = NQ * NZ


def nt(a, b):
    return lax.dot_general(a, b, (((1,), (1,)), ((), ())), preferred_element_type=F32)


def nn(a, b):
    return lax.dot_general(a, b, (((1,), (0,)), ((), ())), preferred_element_type=F32)


def tn(a, b):
    return lax.dot_general(a, b, (((0,), (0,)), ((), ())), preferred_element_type=F32)


def kernel(
    clip_hbm, video_hbm, w1_hbm, w2_hbm, cot_hbm,
    enc_ref, held,
    clip_ref, w1_ref, w2_ref, cot_ref,
    vown, vhalo, coth, flags, flagh, uown, usend, urecv, pre, dsext,
    masks, part, send1, recv1, tiles, recv2, final,
    sin, ra_video, sems, known,
):
    me = lax.axis_index("tm")
    chan = lax.axis_index("chan")
    z, q = me // NQ, lax.rem(me, NQ)
    prev = (lax.rem(me + NT - 1, NT), chan)
    nxt = (lax.rem(me + 1, NT), chan)

    def in_z(s):
        return (z * NQ + lax.rem(q + s, NQ), chan)

    def over_z(s):
        return (lax.rem(z + s, NZ) * NQ + q, chan)

    def over_x(s):
        return (me, lax.rem(chan + s, NX))

    def block(c, size):
        return pl.ds(pl.multiple_of(c * size, size), size)

    def remote(src, dst, ssem, rsem, device):
        return pltpu.make_async_remote_copy(
            src_ref=src, dst_ref=dst, send_sem=ssem, recv_sem=rsem,
            device_id=device, device_id_type=MESH,
        )

    def arrived(semaphore, buffer):
        pltpu.make_async_copy(buffer, buffer, semaphore).wait()

    (s_video, r_behind, s_w, r_w, s_wc, r_wc, s_halo, r_halo, s_cot, r_cot, s_flag, r_flag, s_unit, r_unit,
     s_dhalo, r_dhalo, s_a, r_a, s_b, r_b, s_c, r_c, s_d, r_d) = (sems.at[i] for i in range(24))
    sibling = (me + 1 - 2 * lax.rem(me, 2), chan)

    barrier = pltpu.get_barrier_semaphore()
    near = [over_x(s) for s in range(1, NX)] + [prev, nxt, over_z(1), over_z(NZ - 1)]
    near += [in_z(s) for s in range(1, NQ)]
    for device in near:
        pl.semaphore_signal(barrier, inc=1, device_id=device, device_id_type=MESH)

    own, mine64 = block(chan, 32), block(chan, 64)
    fetch = [
        pltpu.make_async_copy(src, dst, sin.at[i])
        for i, (src, dst) in enumerate([
            (clip_hbm, clip_ref), (cot_hbm, cot_ref), (w2_hbm, w2_ref), (w1_hbm, w1_ref.at[:, mine64]),
            (video_hbm, vown.at[:, own]),
        ])
    ]
    for copy in fetch:
        copy.start()
    fetch[0].wait()

    start = [clip_ref[t] - 4 * me for t in range(4)]
    start2 = [lax.shift_right_arithmetic(clip_ref[2 * j], 1) - 2 * me for j in range(2)]

    def flag(condition):
        return jnp.where(condition, 1.0, 0.0).astype(F32)

    rows = [start2[0] <= -1, start2[0] == -1, start2[0] <= -2, start2[1] <= -1]
    flags[...] = jnp.concatenate(
        [jnp.full((1, 512), flag(r), F32) for r in rows] + [jnp.zeros((12, 512), F32)], axis=0
    ).astype(BF16)

    pl.semaphore_wait(barrier, len(near))

    for s in range(1, NX):
        remote(video_hbm.at[2:4], vown.at[2:4, own], s_video, ra_video.at[s], over_x(s)).start()
    remote(video_hbm.at[2:4], vhalo.at[:, own], s_halo, r_halo, nxt).start()
    core = lax.rem(me, 2)
    w_half = w1_hbm.at[:, block(core, 32)]

    def w_place(c):
        return w1_ref.at[:, block(2 * c + core, 32)]

    for s in range(1, NX):
        remote(w_half, w_place(chan), s_w, r_w, over_x(s)).start()
    for s in range(1, NX):
        remote(video_hbm.at[0:2], vown.at[0:2, own], s_video, r_behind, over_x(s)).start()
    remote(cot_hbm, coth, s_cot, r_cot, prev).start()
    remote(flags, flagh, s_flag, r_flag, prev).start()

    def greet(step, distance):
        for s in (distance, NZ - distance):
            pl.semaphore_signal(known.at[step], inc=1, device_id=over_z(s), device_id_type=MESH)

    greet(0, 1)

    for copy in fetch[1:]:
        copy.wait()

    def masked(x, condition):
        return x * flag(condition).astype(BF16)

    cot = [cot_ref[0], cot_ref[1]]
    masks[0] = masked(cot[0], start2[0] == 0)
    masks[1] = masked(cot[1], start2[1] == 1)
    masks[2] = masked(cot[1], start2[1] <= 0)
    masks[3] = masked(cot[1], start2[1] == 0)
    a, b, c, d = (masks[i] for i in range(4))
    w2 = [w2_ref[k] for k in range(3)]
    local0 = nn(
        jnp.concatenate([w2[0], w2[1], w2[1], w2[2], w2[2]], axis=1),
        jnp.concatenate([cot[0], a, c, a, d], axis=0),
    )
    local1 = nn(
        jnp.concatenate([w2[0], w2[1], w2[2]], axis=1), jnp.concatenate([cot[1], b, b], axis=0)
    )
    arrived(r_cot, coth)
    arrived(r_flag, flagh)
    for i in range(4):
        masks[4 + i] = coth[i // 3] * flagh[i : i + 1, :]
    e, f, g, h = (masks[4 + i] for i in range(4))
    units = [
        local0 + nn(w2[2], g),
        local1 + nn(jnp.concatenate([w2[1], w2[2], w2[2]], axis=1), jnp.concatenate([e, f, h], axis=0)),
    ]
    for i in range(2):
        for x in range(NX):
            piece = units[i][64 * x : 64 * x + 64]
            uown[x, i] = piece
            usend[x, i] = piece.astype(BF16)

    for s in range(1, NX):
        remote(usend.at[lax.rem(chan + s, NX)], urecv.at[s], s_unit, r_unit, over_x(s)).start()

    pl.semaphore_wait(known.at[0], 2)
    greet(1, 2)

    for s in range(1, NX):
        from_s = block(lax.rem(chan + NX - s, NX), 32)
        arrived(ra_video.at[s], vown.at[2:4, from_s])
        remote(vown.at[2:4, from_s], vhalo.at[:, from_s], s_halo, r_halo, nxt).start()
    arrived(r_w, w1_ref.at[:, 0:96])
    for s in range(1, NX):
        part_w = w_place(lax.rem(chan + NX - s, NX))
        remote(part_w, part_w, s_wc, r_wc, sibling).start()
    pl.semaphore_wait(known.at[1], 2)
    greet(2, 4)

    arrived(r_behind, vown.at[0:2, 0:96])
    arrived(r_wc, w1_ref.at[:, 0:96])
    w1 = jnp.concatenate([w1_ref[k] for k in range(3)], axis=1)

    def source(t, k):
        if k == 0:
            return vown[t]
        index = jnp.maximum(t - k, start[t])
        inside = vown[jnp.maximum(index, 0)]
        if t >= k:
            return inside
        return jnp.where(index < 0, vhalo[jnp.clip(index + 2, 0, 1)], inside)

    for j in (1, 0):
        if j == 0:
            arrived(r_halo, vhalo)
        total = None
        for t in (2 * j, 2 * j + 1):
            p = nn(w1, jnp.concatenate([source(t, k) for k in range(3)], axis=0))
            pre[t] = p
            act = p * jax.nn.sigmoid(p)
            total = act if total is None else total + act
        dsext[2 + j] = (0.5 * total).astype(BF16)

    def hand_over(piece):
        send1[piece] = part[piece].astype(BF16)
        s = lax.rem(piece + NQ - q, NQ)

        @pl.when(s != 0)
        def _():
            remote(send1.at[piece], recv1.at[s], s_a, r_a, (z * NQ + piece, chan)).start()

    cot = [cot_ref.at[0], cot_ref.at[1]]
    a, b, c, d, e, f, g, h = (masks.at[i] for i in range(8))
    terms = [
        [(0, cot[0]), (1, cot[1])],
        [(0, a), (1, b), (0, c), (1, e)],
        [(0, a), (1, b), (0, d), (1, f), (0, g), (1, h)],
    ]

    @pl.loop(0, 2)
    def _(half):
        for k in range(3):
            right = jnp.concatenate([v[...] for _, v in terms[k]], axis=1)
            left = [dsext[2 + i, block(half, 128), :] for i, _ in terms[k]]
            part[2 * k + half] = nt(jnp.concatenate(left, axis=1), right)
            hand_over(2 * k + half)

    unit = uown[chan]
    arrived(r_unit, urecv.at[1:NX])
    for s in range(1, NX):
        unit = unit + urecv[s].astype(F32)
    deltas = []
    for t in range(4):
        p = pre[t, mine64, :]
        sig = jax.nn.sigmoid(p)
        deltas.append((0.5 * unit[t // 2] * sig * (1.0 + p * (1.0 - sig))).astype(BF16))
    delta = jnp.concatenate(deltas, axis=1)
    for k in range(3):
        grad = nt(delta, jnp.concatenate([source(t, k) for t in range(4)], axis=1))
        part[6 + k // 2, 64 * (k % 2) : 64 * (k % 2) + 64, :] = grad
    part[7, 64:128, :] = jnp.zeros((64, 128), F32)
    hand_over(6)
    hand_over(7)
    remote(dsext.at[2:4], dsext.at[0:2], s_dhalo, r_dhalo, nxt).start()
    pl.semaphore_wait(known.at[2], 2)

    total = part[q]
    arrived(r_a, recv1.at[1:NQ])
    for s in range(1, NQ):
        total = total + recv1[s].astype(F32)
    tiles[...] = total.astype(BF16).reshape(8, 16, 128)

    owner = lax.rem(z + q, 2) == 0
    mine = z // 2

    def tile_of(s):
        return lax.rem(z + s, NZ) // 2

    def to_owner(s):
        return remote(tiles.at[tile_of(s)], recv2.at[s], s_b, r_b, over_z(s))

    def from_owner(s):
        return remote(final.at[mine], final.at[mine], s_c, r_c, over_z(s))

    @pl.when(owner)
    def _():
        for s in range(2, NZ, 2):
            to_owner(s).start()

    @pl.when(jnp.logical_not(owner))
    def _():
        for s in range(1, NZ, 2):
            to_owner(s).start()

    arrived(r_dhalo, dsext.at[0:2])
    w2t = jnp.concatenate([w2_ref[k] for k in range(3)], axis=0)
    for j in range(2):
        sources = [dsext[jnp.maximum(j - k, start2[j]) + 2] for k in range(3)]
        enc_ref[j] = tn(w2t, jnp.concatenate(sources, axis=0)).astype(BF16)

    @pl.when(owner)
    def _():
        arrived(r_b, recv2.at[1:NZ])
        total = tiles[mine].astype(F32)
        for s in range(1, NZ):
            total = total + recv2[s].astype(F32)
        final[mine] = total.astype(BF16)
        for s in range(1, NZ):
            from_owner(s).start()
        arrived(r_c, recv2.at[0:7])
        arrived(s_b, recv2.at[0:7])
        arrived(s_c, recv2.at[1:NZ])

    @pl.when(jnp.logical_not(owner))
    def _():
        arrived(r_c, recv2.at[0:8])
        arrived(s_b, recv2.at[0:8])

    held[q] = final[...].reshape(128, 128)
    for s in range(1, NQ):
        remote(held.at[q], held.at[q], s_d, r_d, in_z(s)).start()
    arrived(s_video, usend.at[0:3])
    arrived(s_w, w1_ref.at[:, 0:96])
    arrived(s_wc, w1_ref.at[:, 0:96])
    arrived(s_halo, vhalo)
    arrived(s_cot, coth)
    arrived(s_flag, flagh)
    arrived(s_unit, usend.at[0:3])
    arrived(s_dhalo, dsext.at[0:2])
    arrived(s_a, recv1.at[1:NQ])
    arrived(r_d, held.at[1:NQ])
    arrived(s_d, held.at[1:NQ])


def write_kernel(enc_ref, held, out_hbm, o1_hbm, o2_hbm, o1_ref, o2_ref, sems):
    copies = [
        pltpu.make_async_copy(src, dst, sems.at[i])
        for i, (src, dst) in enumerate([(enc_ref, out_hbm), (o1_ref, o1_hbm), (o2_ref, o2_hbm)])
    ]
    copies[0].start()
    for k in range(3):
        o2_ref[k] = held[2 * k : 2 * k + 2].reshape(256, 128).astype(F32) * (131072.0 ** -0.5)
    copies[2].start()
    for k in range(3):
        piece = held[6 + k // 2, (k % 2) * 64 : (k % 2) * 64 + 64, :]
        o1_ref[k] = piece.astype(F32) * (262144.0 ** -0.5)
    copies[1].start()
    for copy in copies:
        copy.wait()


def per_device(video, clip_start, first_conv_weight, second_conv_weight, cotangent):
    vmem = pl.BlockSpec(memory_space=pltpu.VMEM)
    hbm = pl.BlockSpec(memory_space=pltpu.HBM)
    dma = pltpu.SemaphoreType.DMA
    encoded, held = pl.pallas_call(
        kernel,
        out_shape=(
            jax.ShapeDtypeStruct((2, 128, 512), BF16),
            jax.ShapeDtypeStruct((NQ, 128, 128), BF16),
        ),
        in_specs=[hbm] * 5,
        out_specs=(vmem, vmem),
        scratch_shapes=[
            pltpu.SMEM((4,), jnp.int32),
            pltpu.VMEM((3, 256, 128), BF16),
            pltpu.VMEM((3, 256, 128), BF16),
            pltpu.VMEM((2, 128, 512), BF16),
            pltpu.VMEM((4, 128, 512), BF16),
            pltpu.VMEM((2, 128, 512), BF16),
            pltpu.VMEM((2, 128, 512), BF16),
            pltpu.VMEM((16, 512), BF16),
            pltpu.VMEM((16, 512), BF16),
            pltpu.VMEM((NX, 2, 64, 512), F32),
            pltpu.VMEM((NX, 2, 64, 512), BF16),
            pltpu.VMEM((NX, 2, 64, 512), BF16),
            pltpu.VMEM((4, 256, 512), F32),
            pltpu.VMEM((4, 256, 512), BF16),
            pltpu.VMEM((8, 128, 512), BF16),
            pltpu.VMEM((NQ, 128, 128), F32),
            pltpu.VMEM((NQ, 128, 128), BF16),
            pltpu.VMEM((NQ, 128, 128), BF16),
            pltpu.VMEM((8, 16, 128), BF16),
            pltpu.VMEM((NZ, 16, 128), BF16),
            pltpu.VMEM((8, 16, 128), BF16),
            dma((5,)),
            dma((NX,)),
            dma((24,)),
            pltpu.SemaphoreType.REGULAR((3,)),
        ],
        compiler_params=pltpu.CompilerParams(
            collective_id=0, has_side_effects=True, vmem_limit_bytes=40 * 1024 * 1024
        ),
    )(*(
        pltpu.with_memory_space_constraint(x, pltpu.HBM)
        for x in (clip_start, video, first_conv_weight.transpose(0, 2, 1), second_conv_weight, cotangent)
    ))
    encoded, first_grad, second_grad = pl.pallas_call(
        write_kernel,
        out_shape=(
            jax.ShapeDtypeStruct((2, 128, 512), BF16),
            jax.ShapeDtypeStruct((3, 64, 128), F32),
            jax.ShapeDtypeStruct((3, 256, 128), F32),
        ),
        in_specs=[vmem] * 2,
        out_specs=(hbm,) * 3,
        scratch_shapes=[pltpu.VMEM((3, 64, 128), F32), pltpu.VMEM((3, 256, 128), F32), dma((3,))],
        compiler_params=pltpu.CompilerParams(vmem_limit_bytes=8 * 1024 * 1024),
    )(*(pltpu.with_memory_space_constraint(x, pltpu.VMEM) for x in (encoded, held)))
    return encoded, first_grad.transpose(0, 2, 1), second_grad


def solution(mesh):
    in_specs = (
        P("tm", "chan", None),
        P("tm"),
        P(None, None, "chan"),
        P(None, None, "chan"),
        P("tm", "chan", None),
    )
    out_specs = (P("tm", "chan", None), P(None, None, "chan"), P(None, None, "chan"))
    return jax.shard_map(
        per_device, mesh=mesh, in_specs=in_specs, out_specs=out_specs, check_vma=False
    )
```

```python
import jax
import jax.numpy as jnp
from jax import lax
from jax.experimental import pallas as pl
from jax.experimental.pallas import tpu as pltpu
from jax.sharding import PartitionSpec as P

MESH = pl.DeviceIdType.MESH
F32 = jnp.float32
BF16 = jnp.bfloat16
NQ = 8
NZ = 16
NX = 4
NT = NQ * NZ


def nt(a, b):
    return lax.dot_general(a, b, (((1,), (1,)), ((), ())), preferred_element_type=F32)


def nn(a, b):
    return lax.dot_general(a, b, (((1,), (0,)), ((), ())), preferred_element_type=F32)


def tn(a, b):
    return lax.dot_general(a, b, (((0,), (0,)), ((), ())), preferred_element_type=F32)


def kernel(
    clip_hbm, video_hbm, w1_hbm, w2_hbm, cot_hbm,
    enc_ref, held,
    clip_ref, w1_ref, w2_ref, cot_ref,
    vown, vhalo, coth, flags, flagh, uown, usend, urecv, pre, dsext,
    masks, part, send1, recv1, tiles, recv2, final,
    sin, ra_video, sems, known,
):
    me = lax.axis_index("tm")
    chan = lax.axis_index("chan")
    z, q = me // NQ, lax.rem(me, NQ)
    prev = (lax.rem(me + NT - 1, NT), chan)
    nxt = (lax.rem(me + 1, NT), chan)

    def in_z(s):
        return (z * NQ + lax.rem(q + s, NQ), chan)

    def over_z(s):
        return (lax.rem(z + s, NZ) * NQ + q, chan)

    def over_x(s):
        return (me, lax.rem(chan + s, NX))

    def block(c, size):
        return pl.ds(pl.multiple_of(c * size, size), size)

    def remote(src, dst, ssem, rsem, device):
        return pltpu.make_async_remote_copy(
            src_ref=src, dst_ref=dst, send_sem=ssem, recv_sem=rsem,
            device_id=device, device_id_type=MESH,
        )

    def arrived(semaphore, buffer):
        pltpu.make_async_copy(buffer, buffer, semaphore).wait()

    (s_video, r_behind, s_w, r_w, s_wc, r_wc, s_halo, r_halo, s_cot, r_cot, s_flag, r_flag, s_unit, r_unit,
     s_dhalo, r_dhalo, s_a, r_a, s_b, r_b, s_c, r_c, s_d, r_d) = (sems.at[i] for i in range(24))
    sibling = (me + 1 - 2 * lax.rem(me, 2), chan)

    barrier = pltpu.get_barrier_semaphore()
    near = [over_x(s) for s in range(1, NX)] + [over_z(1), over_z(NZ - 1)]
    near += [in_z(s) for s in range(1, NQ)]
    for device in near:
        pl.semaphore_signal(barrier, inc=1, device_id=device, device_id_type=MESH)

    @pl.when(q == 0)
    def _():
        pl.semaphore_signal(barrier, inc=1, device_id=prev, device_id_type=MESH)

    @pl.when(q == NQ - 1)
    def _():
        pl.semaphore_signal(barrier, inc=1, device_id=nxt, device_id_type=MESH)

    own, mine64 = block(chan, 32), block(chan, 64)
    fetch = [
        pltpu.make_async_copy(src, dst, sin.at[i])
        for i, (src, dst) in enumerate([
            (clip_hbm, clip_ref), (cot_hbm, cot_ref), (w2_hbm, w2_ref), (w1_hbm, w1_ref.at[:, mine64]),
            (video_hbm, vown.at[:, own]),
        ])
    ]
    for copy in fetch:
        copy.start()
    fetch[0].wait()

    start = [clip_ref[t] - 4 * me for t in range(4)]
    start2 = [lax.shift_right_arithmetic(clip_ref[2 * j], 1) - 2 * me for j in range(2)]

    def flag(condition):
        return jnp.where(condition, 1.0, 0.0).astype(F32)

    rows = [start2[0] <= -1, start2[0] == -1, start2[0] <= -2, start2[1] <= -1]
    flags[...] = jnp.concatenate(
        [jnp.full((1, 512), flag(r), F32) for r in rows] + [jnp.zeros((12, 512), F32)], axis=0
    ).astype(BF16)

    pl.semaphore_wait(barrier, len(near) + 1 - (lax.rem(q, NQ - 1) + NQ - 3) // (NQ - 2))

    for s in (2, 1, 3):
        remote(video_hbm.at[2:4], vown.at[2:4, own], s_video, ra_video.at[s], over_x(s)).start()
    remote(video_hbm.at[2:4], vhalo.at[:, own], s_halo, r_halo, nxt).start()
    core = lax.rem(me, 2)
    w_half = w1_hbm.at[:, block(core, 32)]

    def w_place(c):
        return w1_ref.at[:, block(2 * c + core, 32)]

    for s in (2, 1, 3):
        remote(w_half, w_place(chan), s_w, r_w, over_x(s)).start()
    for s in (2, 1, 3):
        remote(video_hbm.at[0:2], vown.at[0:2, own], s_video, r_behind, over_x(s)).start()
    remote(cot_hbm, coth, s_cot, r_cot, prev).start()
    remote(flags, flagh, s_flag, r_flag, prev).start()

    def greet(step, distance):
        for s in (distance, NZ - distance):
            pl.semaphore_signal(known.at[step], inc=1, device_id=over_z(s), device_id_type=MESH)

    greet(0, 1)

    for copy in fetch[1:]:
        copy.wait()

    def masked(x, condition):
        return x * flag(condition).astype(BF16)

    cot = [cot_ref[0], cot_ref[1]]
    masks[0] = masked(cot[0], start2[0] == 0)
    masks[1] = masked(cot[1], start2[1] == 1)
    masks[2] = masked(cot[1], start2[1] <= 0)
    masks[3] = masked(cot[1], start2[1] == 0)
    a, b, c, d = (masks[i] for i in range(4))
    w2 = [w2_ref[k] for k in range(3)]
    local0 = nn(
        jnp.concatenate([w2[0], w2[1], w2[1], w2[2], w2[2]], axis=1),
        jnp.concatenate([cot[0], a, c, a, d], axis=0),
    )
    local1 = nn(
        jnp.concatenate([w2[0], w2[1], w2[2]], axis=1), jnp.concatenate([cot[1], b, b], axis=0)
    )
    arrived(r_cot, coth)
    arrived(r_flag, flagh)
    for i in range(4):
        masks[4 + i] = coth[i // 3] * flagh[i : i + 1, :]
    e, f, g, h = (masks[4 + i] for i in range(4))
    units = [
        local0 + nn(w2[2], g),
        local1 + nn(jnp.concatenate([w2[1], w2[2], w2[2]], axis=1), jnp.concatenate([e, f, h], axis=0)),
    ]
    for i in range(2):
        for x in range(NX):
            piece = units[i][64 * x : 64 * x + 64]
            uown[x, i] = piece
            usend[x, i] = piece.astype(BF16)

    for s in (2, 1, 3):
        remote(usend.at[lax.rem(chan + s, NX)], urecv.at[s], s_unit, r_unit, over_x(s)).start()

    pl.semaphore_wait(known.at[0], 2)
    greet(1, 2)

    for s in range(1, NX):
        from_s = block(lax.rem(chan + NX - s, NX), 32)
        arrived(ra_video.at[s], vown.at[2:4, from_s])
        remote(vown.at[2:4, from_s], vhalo.at[:, from_s], s_halo, r_halo, nxt).start()
    arrived(r_w, w1_ref.at[:, 0:96])
    for s in range(1, NX):
        part_w = w_place(lax.rem(chan + NX - s, NX))
        remote(part_w, part_w, s_wc, r_wc, sibling).start()
    pl.semaphore_wait(known.at[1], 2)
    greet(2, 4)

    arrived(r_behind, vown.at[0:2, 0:96])
    arrived(r_wc, w1_ref.at[:, 0:96])
    w1 = jnp.concatenate([w1_ref[k] for k in range(3)], axis=1)

    def source(t, k):
        if k == 0:
            return vown[t]
        index = jnp.maximum(t - k, start[t])
        inside = vown[jnp.maximum(index, 0)]
        if t >= k:
            return inside
        return jnp.where(index < 0, vhalo[jnp.clip(index + 2, 0, 1)], inside)

    for j in (1, 0):
        if j == 0:
            arrived(r_halo, vhalo)
        total = None
        for t in (2 * j, 2 * j + 1):
            p = nn(w1, jnp.concatenate([source(t, k) for k in range(3)], axis=0))
            pre[t] = p
            h = 0.5 * p
            act = h + h * jnp.tanh(h)
            total = act if total is None else total + act
        dsext[2 + j] = (0.5 * total).astype(BF16)

    def hand_over(piece):
        send1[piece] = part[piece].astype(BF16)
        s = lax.rem(piece + NQ - q, NQ)

        @pl.when(s != 0)
        def _():
            remote(send1.at[piece], recv1.at[s], s_a, r_a, (z * NQ + piece, chan)).start()

    cot = [cot_ref.at[0], cot_ref.at[1]]
    a, b, c, d, e, f, g, h = (masks.at[i] for i in range(8))
    def stacked(*refs):
        return jnp.concatenate([r[...] for r in refs], axis=0)

    @pl.loop(0, 2)
    def _(half):
        down0 = dsext[2, block(half, 128), :]
        down1 = dsext[3, block(half, 128), :]
        same = nt(down0, stacked(cot[0], a)) + nt(down1, stacked(cot[1], b))
        later = nt(down0, stacked(c, d)) + nt(down1, stacked(e, f))
        last = nt(down0, g[...]) + nt(down1, h[...])
        part[half] = same[:, :128]
        part[2 + half] = same[:, 128:] + later[:, :128]
        part[4 + half] = same[:, 128:] + later[:, 128:] + last
        for k in range(3):
            hand_over(2 * k + half)

    unit = uown[chan]
    arrived(r_unit, urecv.at[1:NX])
    for s in range(1, NX):
        unit = unit + urecv[s].astype(F32)
    deltas = []
    for t in range(4):
        p = pre[t, mine64, :]
        sig = jax.nn.sigmoid(p)
        deltas.append((0.5 * unit[t // 2] * sig * (1.0 + p * (1.0 - sig))).astype(BF16))
    delta = jnp.concatenate(deltas, axis=1)
    for k in range(3):
        grad = nt(delta, jnp.concatenate([source(t, k) for t in range(4)], axis=1))
        part[6 + k // 2, 64 * (k % 2) : 64 * (k % 2) + 64, :] = grad
    part[7, 64:128, :] = jnp.zeros((64, 128), F32)
    hand_over(6)
    hand_over(7)
    remote(dsext.at[2:4], dsext.at[0:2], s_dhalo, r_dhalo, nxt).start()
    pl.semaphore_wait(known.at[2], 2)

    total = part[q]
    arrived(r_a, recv1.at[1:NQ])
    for s in range(1, NQ):
        total = total + recv1[s].astype(F32)
    tiles[...] = total.astype(BF16).reshape(8, 16, 128)

    owner = lax.rem(z + q, 2) == 0
    mine = z // 2

    def tile_of(s):
        return lax.rem(z + s, NZ) // 2

    def to_owner(s):
        return remote(tiles.at[tile_of(s)], recv2.at[s], s_b, r_b, over_z(s))

    def from_owner(s):
        return remote(final.at[mine], final.at[mine], s_c, r_c, over_z(s))

    @pl.when(owner)
    def _():
        for s in (8, 6, 10, 4, 12, 2, 14):
            to_owner(s).start()

    @pl.when(jnp.logical_not(owner))
    def _():
        for s in (7, 9, 5, 11, 3, 13, 1, 15):
            to_owner(s).start()

    arrived(r_dhalo, dsext.at[0:2])
    w2t = jnp.concatenate([w2_ref[k] for k in range(3)], axis=0)
    for j in range(2):
        sources = [dsext[jnp.maximum(j - k, start2[j]) + 2] for k in range(3)]
        enc_ref[j] = tn(w2t, jnp.concatenate(sources, axis=0)).astype(BF16)

    @pl.when(owner)
    def _():
        arrived(r_b, recv2.at[1:NZ])
        total = tiles[mine].astype(F32)
        for s in range(1, NZ):
            total = total + recv2[s].astype(F32)
        final[mine] = total.astype(BF16)
        for s in (8, 7, 9, 6, 10, 5, 11, 4, 12, 3, 13, 2, 14, 1, 15):
            from_owner(s).start()
        arrived(r_c, recv2.at[0:7])
        arrived(s_b, recv2.at[0:7])
        arrived(s_c, recv2.at[1:NZ])

    @pl.when(jnp.logical_not(owner))
    def _():
        arrived(r_c, recv2.at[0:8])
        arrived(s_b, recv2.at[0:8])

    held[q] = final[...].reshape(128, 128)
    for s in (4, 3, 5, 2, 6, 1, 7):
        remote(held.at[q], held.at[q], s_d, r_d, in_z(s)).start()
    arrived(s_video, usend.at[0:3])
    arrived(s_w, w1_ref.at[:, 0:96])
    arrived(s_wc, w1_ref.at[:, 0:96])
    arrived(s_halo, vhalo)
    arrived(s_cot, coth)
    arrived(s_flag, flagh)
    arrived(s_unit, usend.at[0:3])
    arrived(s_dhalo, dsext.at[0:2])
    arrived(s_a, recv1.at[1:NQ])
    arrived(r_d, held.at[1:NQ])
    arrived(s_d, held.at[1:NQ])


def write_kernel(enc_ref, held, out_hbm, o1_hbm, o2_hbm, o1_ref, o2_ref, sems):
    copies = [
        pltpu.make_async_copy(src, dst, sems.at[i])
        for i, (src, dst) in enumerate([(enc_ref, out_hbm), (o1_ref, o1_hbm), (o2_ref, o2_hbm)])
    ]
    copies[0].start()
    for k in range(3):
        o2_ref[k] = held[2 * k : 2 * k + 2].reshape(256, 128).astype(F32) * (131072.0 ** -0.5)
    copies[2].start()
    for k in range(3):
        piece = held[6 + k // 2, (k % 2) * 64 : (k % 2) * 64 + 64, :]
        o1_ref[k] = piece.astype(F32) * (262144.0 ** -0.5)
    copies[1].start()
    for copy in copies:
        copy.wait()


def per_device(video, clip_start, first_conv_weight, second_conv_weight, cotangent):
    vmem = pl.BlockSpec(memory_space=pltpu.VMEM)
    hbm = pl.BlockSpec(memory_space=pltpu.HBM)
    dma = pltpu.SemaphoreType.DMA
    encoded, held = pl.pallas_call(
        kernel,
        out_shape=(
            jax.ShapeDtypeStruct((2, 128, 512), BF16),
            jax.ShapeDtypeStruct((NQ, 128, 128), BF16),
        ),
        in_specs=[hbm] * 5,
        out_specs=(vmem, vmem),
        scratch_shapes=[
            pltpu.SMEM((4,), jnp.int32),
            pltpu.VMEM((3, 256, 128), BF16),
            pltpu.VMEM((3, 256, 128), BF16),
            pltpu.VMEM((2, 128, 512), BF16),
            pltpu.VMEM((4, 128, 512), BF16),
            pltpu.VMEM((2, 128, 512), BF16),
            pltpu.VMEM((2, 128, 512), BF16),
            pltpu.VMEM((16, 512), BF16),
            pltpu.VMEM((16, 512), BF16),
            pltpu.VMEM((NX, 2, 64, 512), F32),
            pltpu.VMEM((NX, 2, 64, 512), BF16),
            pltpu.VMEM((NX, 2, 64, 512), BF16),
            pltpu.VMEM((4, 256, 512), F32),
            pltpu.VMEM((4, 256, 512), BF16),
            pltpu.VMEM((8, 128, 512), BF16),
            pltpu.VMEM((NQ, 128, 128), F32),
            pltpu.VMEM((NQ, 128, 128), BF16),
            pltpu.VMEM((NQ, 128, 128), BF16),
            pltpu.VMEM((8, 16, 128), BF16),
            pltpu.VMEM((NZ, 16, 128), BF16),
            pltpu.VMEM((8, 16, 128), BF16),
            dma((5,)),
            dma((NX,)),
            dma((24,)),
            pltpu.SemaphoreType.REGULAR((3,)),
        ],
        compiler_params=pltpu.CompilerParams(
            collective_id=0, has_side_effects=True, vmem_limit_bytes=40 * 1024 * 1024
        ),
    )(*(
        pltpu.with_memory_space_constraint(x, pltpu.HBM)
        for x in (clip_start, video, first_conv_weight.transpose(0, 2, 1), second_conv_weight, cotangent)
    ))
    encoded, first_grad, second_grad = pl.pallas_call(
        write_kernel,
        out_shape=(
            jax.ShapeDtypeStruct((2, 128, 512), BF16),
            jax.ShapeDtypeStruct((3, 64, 128), F32),
            jax.ShapeDtypeStruct((3, 256, 128), F32),
        ),
        in_specs=[vmem] * 2,
        out_specs=(hbm,) * 3,
        scratch_shapes=[pltpu.VMEM((3, 64, 128), F32), pltpu.VMEM((3, 256, 128), F32), dma((3,))],
        compiler_params=pltpu.CompilerParams(vmem_limit_bytes=8 * 1024 * 1024),
    )(*(pltpu.with_memory_space_constraint(x, pltpu.VMEM) for x in (encoded, held)))
    return encoded, first_grad.transpose(0, 2, 1), second_grad


def solution(mesh):
    in_specs = (
        P("tm", "chan", None),
        P("tm"),
        P(None, None, "chan"),
        P(None, None, "chan"),
        P("tm", "chan", None),
    )
    out_specs = (P("tm", "chan", None), P(None, None, "chan"), P(None, None, "chan"))
    return jax.shard_map(
        per_device, mesh=mesh, in_specs=in_specs, out_specs=out_specs, check_vma=False
    )
```

```python
import jax
import jax.numpy as jnp
from jax import lax
from jax.experimental import pallas as pl
from jax.experimental.pallas import tpu as pltpu
from jax.sharding import PartitionSpec as P

MESH = pl.DeviceIdType.MESH
F32 = jnp.float32
BF16 = jnp.bfloat16
NQ = 8
NZ = 16
NX = 4
NT = NQ * NZ


def nt(a, b):
    return lax.dot_general(a, b, (((1,), (1,)), ((), ())), preferred_element_type=F32)


def nn(a, b):
    return lax.dot_general(a, b, (((1,), (0,)), ((), ())), preferred_element_type=F32)


def tn(a, b):
    return lax.dot_general(a, b, (((0,), (0,)), ((), ())), preferred_element_type=F32)


def kernel(
    clip_hbm, video_hbm, w1_hbm, w2_hbm, cot_hbm,
    enc_ref, held,
    clip_ref, w1_ref, w2_ref, cot_ref,
    vown, vhalo, coth, flags, flagh, uown, usend, urecv, pre, dsext,
    masks, part, send1, recv1, tiles, recv2,
    sin, ra_video, r_c, sems, known,
):
    me = lax.axis_index("tm")
    chan = lax.axis_index("chan")
    z, q = me // NQ, lax.rem(me, NQ)
    prev = (lax.rem(me + NT - 1, NT), chan)
    nxt = (lax.rem(me + 1, NT), chan)

    def in_z(s):
        return (z * NQ + lax.rem(q + s, NQ), chan)

    def over_z(s):
        return (lax.rem(z + s, NZ) * NQ + q, chan)

    def over_x(s):
        return (me, lax.rem(chan + s, NX))

    def block(c, size):
        return pl.ds(pl.multiple_of(c * size, size), size)

    def remote(src, dst, ssem, rsem, device):
        return pltpu.make_async_remote_copy(
            src_ref=src, dst_ref=dst, send_sem=ssem, recv_sem=rsem,
            device_id=device, device_id_type=MESH,
        )

    def arrived(semaphore, buffer):
        pltpu.make_async_copy(buffer, buffer, semaphore).wait()

    (s_video, r_behind, s_w, r_w, s_wc, r_wc, s_halo, r_halo, s_cot, r_cot, s_flag, r_flag, s_unit, r_unit,
     s_dhalo, r_dhalo, s_a, r_a, s_b, r_b, s_c, s_d, r_d) = (sems.at[i] for i in range(23))
    sibling = (me + 1 - 2 * lax.rem(me, 2), chan)

    barrier = pltpu.get_barrier_semaphore()
    near = [over_x(s) for s in range(1, NX)] + [over_z(1), over_z(NZ - 1)]
    near += [in_z(s) for s in range(1, NQ)]
    for device in near:
        pl.semaphore_signal(barrier, inc=1, device_id=device, device_id_type=MESH)

    @pl.when(q == 0)
    def _():
        pl.semaphore_signal(barrier, inc=1, device_id=prev, device_id_type=MESH)

    @pl.when(q == NQ - 1)
    def _():
        pl.semaphore_signal(barrier, inc=1, device_id=nxt, device_id_type=MESH)

    own, mine64 = block(chan, 32), block(chan, 64)
    fetch = [
        pltpu.make_async_copy(src, dst, sin.at[i])
        for i, (src, dst) in enumerate([
            (clip_hbm, clip_ref), (cot_hbm, cot_ref), (w2_hbm, w2_ref), (w1_hbm, w1_ref.at[:, mine64]),
            (video_hbm, vown.at[:, own]),
        ])
    ]
    for copy in fetch:
        copy.start()
    fetch[0].wait()

    start = [clip_ref[t] - 4 * me for t in range(4)]
    start2 = [lax.shift_right_arithmetic(clip_ref[2 * j], 1) - 2 * me for j in range(2)]

    def flag(condition):
        return jnp.where(condition, 1.0, 0.0).astype(F32)

    rows = [start2[0] <= -1, start2[0] == -1, start2[0] <= -2, start2[1] <= -1]
    flags[...] = jnp.concatenate(
        [jnp.full((1, 512), flag(r), F32) for r in rows] + [jnp.zeros((12, 512), F32)], axis=0
    ).astype(BF16)

    pl.semaphore_wait(barrier, len(near) + 1 - (lax.rem(q, NQ - 1) + NQ - 3) // (NQ - 2))

    for s in (2, 1, 3):
        remote(video_hbm.at[2:4], vown.at[2:4, own], s_video, ra_video.at[s], over_x(s)).start()
    remote(video_hbm.at[2:4], vhalo.at[:, own], s_halo, r_halo, nxt).start()
    core = lax.rem(me, 2)
    w_half = w1_hbm.at[:, block(core, 32)]

    def w_place(c):
        return w1_ref.at[:, block(2 * c + core, 32)]

    for s in (2, 1, 3):
        remote(w_half, w_place(chan), s_w, r_w, over_x(s)).start()
    for s in (2, 1, 3):
        remote(video_hbm.at[0:2], vown.at[0:2, own], s_video, r_behind, over_x(s)).start()
    remote(cot_hbm, coth, s_cot, r_cot, prev).start()
    remote(flags, flagh, s_flag, r_flag, prev).start()

    def greet(step, distance):
        for s in (distance, NZ - distance):
            pl.semaphore_signal(known.at[step], inc=1, device_id=over_z(s), device_id_type=MESH)

    greet(0, 1)

    for copy in fetch[1:]:
        copy.wait()

    def masked(x, condition):
        return x * flag(condition).astype(BF16)

    cot = [cot_ref[0], cot_ref[1]]
    masks[0] = masked(cot[0], start2[0] == 0)
    masks[1] = masked(cot[1], start2[1] == 1)
    masks[2] = masked(cot[1], start2[1] <= 0)
    masks[3] = masked(cot[1], start2[1] == 0)
    a, b, c, d = (masks[i] for i in range(4))
    w2 = [w2_ref[k] for k in range(3)]
    local0 = nn(
        jnp.concatenate([w2[0], w2[1], w2[1], w2[2], w2[2]], axis=1),
        jnp.concatenate([cot[0], a, c, a, d], axis=0),
    )
    local1 = nn(
        jnp.concatenate([w2[0], w2[1], w2[2]], axis=1), jnp.concatenate([cot[1], b, b], axis=0)
    )
    arrived(r_cot, coth)
    arrived(r_flag, flagh)
    for i in range(4):
        masks[4 + i] = coth[i // 3] * flagh[i : i + 1, :]
    e, f, g, h = (masks[4 + i] for i in range(4))
    units = [
        local0 + nn(w2[2], g),
        local1 + nn(jnp.concatenate([w2[1], w2[2], w2[2]], axis=1), jnp.concatenate([e, f, h], axis=0)),
    ]
    for i in range(2):
        for x in range(NX):
            piece = units[i][64 * x : 64 * x + 64]
            uown[x, i] = piece
            usend[x, i] = piece.astype(BF16)

    for s in (2, 1, 3):
        remote(usend.at[lax.rem(chan + s, NX)], urecv.at[s], s_unit, r_unit, over_x(s)).start()

    pl.semaphore_wait(known.at[0], 2)
    greet(1, 2)

    for s in range(1, NX):
        from_s = block(lax.rem(chan + NX - s, NX), 32)
        arrived(ra_video.at[s], vown.at[2:4, from_s])
        remote(vown.at[2:4, from_s], vhalo.at[:, from_s], s_halo, r_halo, nxt).start()
    arrived(r_w, w1_ref.at[:, 0:96])
    for s in range(1, NX):
        part_w = w_place(lax.rem(chan + NX - s, NX))
        remote(part_w, part_w, s_wc, r_wc, sibling).start()
    pl.semaphore_wait(known.at[1], 2)
    greet(2, 4)

    arrived(r_behind, vown.at[0:2, 0:96])
    arrived(r_wc, w1_ref.at[:, 0:96])
    w1 = jnp.concatenate([w1_ref[k] for k in range(3)], axis=1)

    def source(t, k):
        if k == 0:
            return vown[t]
        index = jnp.maximum(t - k, start[t])
        inside = vown[jnp.maximum(index, 0)]
        if t >= k:
            return inside
        return jnp.where(index < 0, vhalo[jnp.clip(index + 2, 0, 1)], inside)

    for j in (1, 0):
        if j == 0:
            arrived(r_halo, vhalo)
        total = None
        for t in (2 * j, 2 * j + 1):
            p = nn(w1, jnp.concatenate([source(t, k) for k in range(3)], axis=0))
            pre[t] = p
            h = 0.5 * p
            act = h + h * jnp.tanh(h)
            total = act if total is None else total + act
        dsext[2 + j] = (0.5 * total).astype(BF16)

    def hand_over(piece):
        send1[piece] = part[piece].astype(BF16)
        s = lax.rem(piece + NQ - q, NQ)

        @pl.when(s != 0)
        def _():
            remote(send1.at[piece], recv1.at[s], s_a, r_a, (z * NQ + piece, chan)).start()

    cot = [cot_ref.at[0], cot_ref.at[1]]
    a, b, c, d, e, f, g, h = (masks.at[i] for i in range(8))
    def stacked(*refs):
        return jnp.concatenate([r[...] for r in refs], axis=0)

    @pl.loop(0, 2)
    def _(half):
        down0 = dsext[2, block(half, 128), :]
        down1 = dsext[3, block(half, 128), :]
        same = nt(down0, stacked(cot[0], a)) + nt(down1, stacked(cot[1], b))
        later = nt(down0, stacked(c, d)) + nt(down1, stacked(e, f))
        last = nt(down0, g[...]) + nt(down1, h[...])
        part[half] = same[:, :128]
        part[2 + half] = same[:, 128:] + later[:, :128]
        part[4 + half] = same[:, 128:] + later[:, 128:] + last
        for k in range(3):
            hand_over(2 * k + half)

    unit = uown[chan]
    arrived(r_unit, urecv.at[1:NX])
    for s in range(1, NX):
        unit = unit + urecv[s].astype(F32)
    deltas = []
    for t in range(4):
        p = pre[t, mine64, :]
        sig = jax.nn.sigmoid(p)
        deltas.append((0.5 * unit[t // 2] * sig * (1.0 + p * (1.0 - sig))).astype(BF16))
    delta = jnp.concatenate(deltas, axis=1)
    for k in range(3):
        grad = nt(delta, jnp.concatenate([source(t, k) for t in range(4)], axis=1))
        part[6 + k // 2, 64 * (k % 2) : 64 * (k % 2) + 64, :] = grad
    part[7, 64:128, :] = jnp.zeros((64, 128), F32)
    hand_over(6)
    hand_over(7)
    remote(dsext.at[2:4], dsext.at[0:2], s_dhalo, r_dhalo, nxt).start()
    pl.semaphore_wait(known.at[2], 2)

    total = part[q]
    arrived(r_a, recv1.at[1:NQ])
    for s in range(1, NQ):
        total = total + recv1[s].astype(F32)
    tiles[...] = total.astype(BF16).reshape(8, 16, 128)

    owner = lax.rem(z + q, 2) == 0
    mine = z // 2

    def tile_of(s):
        return lax.rem(z + s, NZ) // 2

    def to_owner(s):
        return remote(tiles.at[tile_of(s)], recv2.at[s], s_b, r_b, over_z(s))

    def slot_at(there):
        return lax.rem(mine + 10 - (there + 1) // 2, 8)

    def from_owner(s):
        slot = slot_at(lax.rem(z + s, NZ))
        return remote(held.at[q, slot_at(z)], held.at[q, slot], s_c, r_c.at[slot // 4], over_z(s))

    def spread(part_of):
        for s in (4, 3, 5, 2, 6, 1, 7):
            remote(held.at[q, part_of], held.at[q, part_of], s_d, r_d, in_z(s)).start()

    @pl.when(owner)
    def _():
        for s in (8, 6, 10, 4, 12, 2, 14):
            to_owner(s).start()

    @pl.when(jnp.logical_not(owner))
    def _():
        for s in (7, 9, 5, 11, 3, 13, 1, 15):
            to_owner(s).start()

    arrived(r_dhalo, dsext.at[0:2])
    w2t = jnp.concatenate([w2_ref[k] for k in range(3)], axis=0)
    for j in range(2):
        sources = [dsext[jnp.maximum(j - k, start2[j]) + 2] for k in range(3)]
        enc_ref[j] = tn(w2t, jnp.concatenate(sources, axis=0)).astype(BF16)

    @pl.when(owner)
    def _():
        arrived(r_b, recv2.at[1:NZ])
        total = tiles[mine].astype(F32)
        for s in range(1, NZ):
            total = total + recv2[s].astype(F32)
        held[q, slot_at(z)] = total.astype(BF16)
        for s in (8, 7, 9, 6, 10, 5, 11, 4, 12, 3, 13, 2, 14, 1, 15):
            from_owner(s).start()
        arrived(r_c.at[0], recv2.at[0:3])
        arrived(s_b, recv2.at[0:7])

    @pl.when(jnp.logical_not(owner))
    def _():
        arrived(r_c.at[0], recv2.at[0:4])
        arrived(s_b, recv2.at[0:8])

    spread(pl.ds(0, 4))
    arrived(r_c.at[1], recv2.at[0:4])
    spread(pl.ds(4, 4))

    @pl.when(owner)
    def _():
        arrived(s_c, recv2.at[1:NZ])

    arrived(s_video, usend.at[0:3])
    arrived(s_w, w1_ref.at[:, 0:96])
    arrived(s_wc, w1_ref.at[:, 0:96])
    arrived(s_halo, vhalo)
    arrived(s_cot, coth)
    arrived(s_flag, flagh)
    arrived(s_unit, usend.at[0:3])
    arrived(s_dhalo, dsext.at[0:2])
    arrived(s_a, recv1.at[1:NQ])
    arrived(r_d, held.at[1:NQ])
    arrived(s_d, held.at[1:NQ])


def write_kernel(enc_ref, held, out_hbm, o1_hbm, o2_hbm, o1_ref, o2_ref, sems):
    copies = [
        pltpu.make_async_copy(src, dst, sems.at[i])
        for i, (src, dst) in enumerate([(enc_ref, out_hbm), (o1_ref, o1_hbm), (o2_ref, o2_hbm)])
    ]
    copies[0].start()
    shift = 10 - (lax.axis_index("tm") // NQ + 1) // 2

    def tile(piece, i):
        return held[piece, lax.rem(i + shift, 8)].astype(F32)

    for piece in range(6):
        for i in range(8):
            rows = slice(128 * (piece % 2) + 16 * i, 128 * (piece % 2) + 16 * i + 16)
            o2_ref[piece // 2, rows, :] = tile(piece, i) * (131072.0 ** -0.5)
    copies[2].start()
    for k in range(3):
        for i in range(4):
            part = tile(6 + k // 2, 4 * (k % 2) + i)
            o1_ref[k, 16 * i : 16 * i + 16, :] = part * (262144.0 ** -0.5)
    copies[1].start()
    for copy in copies:
        copy.wait()


def per_device(video, clip_start, first_conv_weight, second_conv_weight, cotangent):
    vmem = pl.BlockSpec(memory_space=pltpu.VMEM)
    hbm = pl.BlockSpec(memory_space=pltpu.HBM)
    dma = pltpu.SemaphoreType.DMA
    encoded, held = pl.pallas_call(
        kernel,
        out_shape=(
            jax.ShapeDtypeStruct((2, 128, 512), BF16),
            jax.ShapeDtypeStruct((NQ, 8, 16, 128), BF16),
        ),
        in_specs=[hbm] * 5,
        out_specs=(vmem, vmem),
        scratch_shapes=[
            pltpu.SMEM((4,), jnp.int32),
            pltpu.VMEM((3, 256, 128), BF16),
            pltpu.VMEM((3, 256, 128), BF16),
            pltpu.VMEM((2, 128, 512), BF16),
            pltpu.VMEM((4, 128, 512), BF16),
            pltpu.VMEM((2, 128, 512), BF16),
            pltpu.VMEM((2, 128, 512), BF16),
            pltpu.VMEM((16, 512), BF16),
            pltpu.VMEM((16, 512), BF16),
            pltpu.VMEM((NX, 2, 64, 512), F32),
            pltpu.VMEM((NX, 2, 64, 512), BF16),
            pltpu.VMEM((NX, 2, 64, 512), BF16),
            pltpu.VMEM((4, 256, 512), F32),
            pltpu.VMEM((4, 256, 512), BF16),
            pltpu.VMEM((8, 128, 512), BF16),
            pltpu.VMEM((NQ, 128, 128), F32),
            pltpu.VMEM((NQ, 128, 128), BF16),
            pltpu.VMEM((NQ, 128, 128), BF16),
            pltpu.VMEM((8, 16, 128), BF16),
            pltpu.VMEM((NZ, 16, 128), BF16),
            dma((5,)),
            dma((NX,)),
            dma((2,)),
            dma((23,)),
            pltpu.SemaphoreType.REGULAR((3,)),
        ],
        compiler_params=pltpu.CompilerParams(
            collective_id=0, has_side_effects=True, vmem_limit_bytes=40 * 1024 * 1024
        ),
    )(*(
        pltpu.with_memory_space_constraint(x, pltpu.HBM)
        for x in (clip_start, video, first_conv_weight.transpose(0, 2, 1), second_conv_weight, cotangent)
    ))
    encoded, first_grad, second_grad = pl.pallas_call(
        write_kernel,
        out_shape=(
            jax.ShapeDtypeStruct((2, 128, 512), BF16),
            jax.ShapeDtypeStruct((3, 64, 128), F32),
            jax.ShapeDtypeStruct((3, 256, 128), F32),
        ),
        in_specs=[vmem] * 2,
        out_specs=(hbm,) * 3,
        scratch_shapes=[pltpu.VMEM((3, 64, 128), F32), pltpu.VMEM((3, 256, 128), F32), dma((3,))],
        compiler_params=pltpu.CompilerParams(vmem_limit_bytes=8 * 1024 * 1024),
    )(*(pltpu.with_memory_space_constraint(x, pltpu.VMEM) for x in (encoded, held)))
    return encoded, first_grad.transpose(0, 2, 1), second_grad


def solution(mesh):
    in_specs = (
        P("tm", "chan", None),
        P("tm"),
        P(None, None, "chan"),
        P(None, None, "chan"),
        P("tm", "chan", None),
    )
    out_specs = (P("tm", "chan", None), P(None, None, "chan"), P(None, None, "chan"))
    return jax.shard_map(
        per_device, mesh=mesh, in_specs=in_specs, out_specs=out_specs, check_vma=False
    )
```

```python
import jax
import jax.numpy as jnp
from jax import lax
from jax.experimental import pallas as pl
from jax.experimental.pallas import tpu as pltpu
from jax.sharding import PartitionSpec as P

MESH = pl.DeviceIdType.MESH
F32 = jnp.float32
BF16 = jnp.bfloat16
NQ = 8
NZ = 16
NX = 4
NT = NQ * NZ


def nt(a, b):
    return lax.dot_general(a, b, (((1,), (1,)), ((), ())), preferred_element_type=F32)


def nn(a, b):
    return lax.dot_general(a, b, (((1,), (0,)), ((), ())), preferred_element_type=F32)


def tn(a, b):
    return lax.dot_general(a, b, (((0,), (0,)), ((), ())), preferred_element_type=F32)


def kernel(
    clip_hbm, video_hbm, w1_hbm, w2_hbm, cot_hbm,
    enc_ref, held,
    clip_ref, w1_ref, w2_ref, cot_ref,
    vown, vhalo, coth, flags, flagh, uown, usend, urecv, pre, dsext,
    masks, part, send1, recv1, tiles, recv2,
    sin, ra_video, r_c, sems, known,
):
    me = lax.axis_index("tm")
    chan = lax.axis_index("chan")
    z, q = me // NQ, lax.rem(me, NQ)
    prev = (lax.rem(me + NT - 1, NT), chan)
    nxt = (lax.rem(me + 1, NT), chan)

    def in_z(s):
        return (z * NQ + lax.rem(q + s, NQ), chan)

    def over_z(s):
        return (lax.rem(z + s, NZ) * NQ + q, chan)

    def over_x(s):
        return (me, lax.rem(chan + s, NX))

    def block(c, size):
        return pl.ds(pl.multiple_of(c * size, size), size)

    def remote(src, dst, ssem, rsem, device):
        return pltpu.make_async_remote_copy(
            src_ref=src, dst_ref=dst, send_sem=ssem, recv_sem=rsem,
            device_id=device, device_id_type=MESH,
        )

    def arrived(semaphore, buffer):
        pltpu.make_async_copy(buffer, buffer, semaphore).wait()

    (s_video, r_behind, s_w, r_w, s_wc, r_wc, s_halo, r_halo, s_cot, r_cot, s_flag, r_flag, s_unit, r_unit,
     s_dhalo, r_dhalo, s_a, r_a, s_b, r_b, s_c, s_d, r_d) = (sems.at[i] for i in range(23))
    sibling = (me + 1 - 2 * lax.rem(me, 2), chan)

    barrier = pltpu.get_barrier_semaphore()
    near = [over_x(s) for s in range(1, NX)] + [over_z(1), over_z(NZ - 1)]
    near += [in_z(s) for s in range(1, NQ)]
    for device in near:
        pl.semaphore_signal(barrier, inc=1, device_id=device, device_id_type=MESH)

    @pl.when(q == 0)
    def _():
        pl.semaphore_signal(barrier, inc=1, device_id=prev, device_id_type=MESH)

    @pl.when(q == NQ - 1)
    def _():
        pl.semaphore_signal(barrier, inc=1, device_id=nxt, device_id_type=MESH)

    own, mine64 = block(chan, 32), block(chan, 64)
    fetch = [
        pltpu.make_async_copy(src, dst, sin.at[i])
        for i, (src, dst) in enumerate([
            (clip_hbm, clip_ref), (cot_hbm, cot_ref), (w2_hbm, w2_ref), (w1_hbm, w1_ref.at[:, mine64]),
            (video_hbm, vown.at[:, own]),
        ])
    ]
    for copy in fetch:
        copy.start()
    fetch[0].wait()

    start = [clip_ref[t] - 4 * me for t in range(4)]
    start2 = [lax.shift_right_arithmetic(clip_ref[2 * j], 1) - 2 * me for j in range(2)]

    def flag(condition):
        return jnp.where(condition, 1.0, 0.0).astype(F32)

    rows = [start2[0] <= -1, start2[0] == -1, start2[0] <= -2, start2[1] <= -1]
    flags[...] = jnp.concatenate(
        [jnp.full((1, 512), flag(r), F32) for r in rows] + [jnp.zeros((12, 512), F32)], axis=0
    ).astype(BF16)

    pl.semaphore_wait(barrier, len(near) + 1 - (lax.rem(q, NQ - 1) + NQ - 3) // (NQ - 2))

    for s in (2, 1, 3):
        remote(video_hbm.at[2:4], vown.at[2:4, own], s_video, ra_video.at[s], over_x(s)).start()
    remote(video_hbm.at[2:4], vhalo.at[:, own], s_halo, r_halo, nxt).start()
    core = lax.rem(me, 2)
    w_half = w1_hbm.at[:, block(core, 32)]

    def w_place(c):
        return w1_ref.at[:, block(2 * c + core, 32)]

    for s in (2, 1, 3):
        remote(w_half, w_place(chan), s_w, r_w, over_x(s)).start()
    for s in (2, 1, 3):
        remote(video_hbm.at[0:2], vown.at[0:2, own], s_video, r_behind, over_x(s)).start()
    remote(cot_hbm, coth, s_cot, r_cot, prev).start()
    remote(flags, flagh, s_flag, r_flag, prev).start()

    def greet(step, distance):
        for s in (distance, NZ - distance):
            pl.semaphore_signal(known.at[step], inc=1, device_id=over_z(s), device_id_type=MESH)

    greet(0, 1)

    for copy in fetch[1:]:
        copy.wait()

    def masked(x, condition):
        return x * flag(condition).astype(BF16)

    cot = [cot_ref[0], cot_ref[1]]
    masks[0] = masked(cot[0], start2[0] == 0)
    masks[1] = masked(cot[1], start2[1] == 1)
    masks[2] = masked(cot[1], start2[1] <= 0)
    masks[3] = masked(cot[1], start2[1] == 0)
    a, b, c, d = (masks[i] for i in range(4))
    w2 = [w2_ref[k] for k in range(3)]
    local0 = nn(
        jnp.concatenate([w2[0], w2[1], w2[1], w2[2], w2[2]], axis=1),
        jnp.concatenate([cot[0], a, c, a, d], axis=0),
    )
    local1 = nn(
        jnp.concatenate([w2[0], w2[1], w2[2]], axis=1), jnp.concatenate([cot[1], b, b], axis=0)
    )
    arrived(r_cot, coth)
    arrived(r_flag, flagh)
    for i in range(4):
        masks[4 + i] = coth[i // 3] * flagh[i : i + 1, :]
    e, f, g, h = (masks[4 + i] for i in range(4))
    units = [
        local0 + nn(w2[2], g),
        local1 + nn(jnp.concatenate([w2[1], w2[2], w2[2]], axis=1), jnp.concatenate([e, f, h], axis=0)),
    ]
    for i in range(2):
        for x in range(NX):
            piece = units[i][64 * x : 64 * x + 64]
            uown[x, i] = piece
            usend[x, i] = piece.astype(BF16)

    for s in (2, 1, 3):
        remote(usend.at[lax.rem(chan + s, NX)], urecv.at[s], s_unit, r_unit, over_x(s)).start()

    pl.semaphore_wait(known.at[0], 2)
    greet(1, 2)

    for s in range(1, NX):
        from_s = block(lax.rem(chan + NX - s, NX), 32)
        arrived(ra_video.at[s], vown.at[2:4, from_s])
        remote(vown.at[2:4, from_s], vhalo.at[:, from_s], s_halo, r_halo, nxt).start()
    arrived(r_w, w1_ref.at[:, 0:96])
    for s in range(1, NX):
        part_w = w_place(lax.rem(chan + NX - s, NX))
        remote(part_w, part_w, s_wc, r_wc, sibling).start()
    pl.semaphore_wait(known.at[1], 2)
    greet(2, 4)

    arrived(r_behind, vown.at[0:2, 0:96])
    arrived(r_wc, w1_ref.at[:, 0:96])
    w1 = jnp.concatenate([w1_ref[k] for k in range(3)], axis=1)

    def source(t, k):
        if k == 0:
            return vown[t]
        index = jnp.maximum(t - k, start[t])
        inside = vown[jnp.maximum(index, 0)]
        if t >= k:
            return inside
        return jnp.where(index < 0, vhalo[jnp.clip(index + 2, 0, 1)], inside)

    for j in (1, 0):
        if j == 0:
            arrived(r_halo, vhalo)
        total = None
        for t in (2 * j, 2 * j + 1):
            p = nn(w1, jnp.concatenate([source(t, k) for k in range(3)], axis=0))
            pre[t] = p
            h = 0.5 * p
            act = h + h * jnp.tanh(h)
            total = act if total is None else total + act
        dsext[2 + j] = (0.5 * total).astype(BF16)

    def hand_over(piece):
        send1[piece] = part[piece].astype(BF16)
        s = lax.rem(piece + NQ - q, NQ)

        @pl.when(s != 0)
        def _():
            remote(send1.at[piece], recv1.at[s], s_a, r_a, (z * NQ + piece, chan)).start()

    cot = [cot_ref.at[0], cot_ref.at[1]]
    a, b, c, d, e, f, g, h = (masks.at[i] for i in range(8))
    def stacked(*refs):
        return jnp.concatenate([r[...] for r in refs], axis=0)

    @pl.loop(0, 2)
    def _(half):
        down0 = dsext[2, block(half, 128), :]
        down1 = dsext[3, block(half, 128), :]
        same = nt(down0, stacked(cot[0], a)) + nt(down1, stacked(cot[1], b))
        later = nt(down0, stacked(c, d)) + nt(down1, stacked(e, f))
        last = nt(down0, g[...]) + nt(down1, h[...])
        part[half] = same[:, :128]
        part[2 + half] = same[:, 128:] + later[:, :128]
        part[4 + half] = same[:, 128:] + later[:, 128:] + last
        for k in range(3):
            hand_over(2 * k + half)

    unit = uown[chan]
    arrived(r_unit, urecv.at[1:NX])
    for s in range(1, NX):
        unit = unit + urecv[s].astype(F32)
    deltas = []
    for t in range(4):
        p = pre[t, mine64, :]
        sig = jax.nn.sigmoid(p)
        deltas.append((0.5 * unit[t // 2] * sig * (1.0 + p * (1.0 - sig))).astype(BF16))
    delta = jnp.concatenate(deltas, axis=1)
    for k in range(3):
        grad = nt(delta, jnp.concatenate([source(t, k) for t in range(4)], axis=1))
        part[6 + k // 2, 64 * (k % 2) : 64 * (k % 2) + 64, :] = grad
    part[7, 64:128, :] = jnp.zeros((64, 128), F32)
    hand_over(6)
    hand_over(7)
    remote(dsext.at[2:4], dsext.at[0:2], s_dhalo, r_dhalo, nxt).start()
    pl.semaphore_wait(known.at[2], 2)

    total = part[q]
    arrived(r_a, recv1.at[1:NQ])
    for s in range(1, NQ):
        total = total + recv1[s].astype(F32)
    tiles[...] = total.astype(BF16).reshape(8, 16, 128)

    owner = lax.rem(z + q, 2) == 0
    mine = z // 2

    def tile_of(s):
        return lax.rem(z + s, NZ) // 2

    def to_owner(s):
        return remote(tiles.at[tile_of(s)], recv2.at[s], s_b, r_b, over_z(s))

    def slot_at(there):
        return lax.rem(mine + 10 - (there + 1) // 2, 8)

    def from_owner(s):
        slot = slot_at(lax.rem(z + s, NZ))
        return remote(held.at[q, slot_at(z)], held.at[q, slot], s_c, r_c.at[slot // 4], over_z(s))

    def spread(part_of):
        for s in (4, 3, 5, 2, 6, 1, 7):
            remote(held.at[q, part_of], held.at[q, part_of], s_d, r_d, in_z(s)).start()

    @pl.when(owner)
    def _():
        for s in (8, 6, 10, 4, 12, 2, 14):
            to_owner(s).start()

    @pl.when(jnp.logical_not(owner))
    def _():
        for s in (7, 9, 5, 11, 3, 13, 1, 15):
            to_owner(s).start()

    @pl.when(owner)
    def _():
        arrived(r_b, recv2.at[1:NZ])
        total = tiles[mine].astype(F32)
        for s in range(1, NZ):
            total = total + recv2[s].astype(F32)
        held[q, slot_at(z)] = total.astype(BF16)
        for s in (8, 7, 9, 6, 10, 5, 11, 4, 12, 3, 13, 2, 14, 1, 15):
            from_owner(s).start()

    arrived(r_dhalo, dsext.at[0:2])
    w2t = jnp.concatenate([w2_ref[k] for k in range(3)], axis=0)
    for j in range(2):
        sources = [dsext[jnp.maximum(j - k, start2[j]) + 2] for k in range(3)]
        enc_ref[j] = tn(w2t, jnp.concatenate(sources, axis=0)).astype(BF16)

    @pl.when(owner)
    def _():
        arrived(r_c.at[0], recv2.at[0:3])
        arrived(s_b, recv2.at[0:7])

    @pl.when(jnp.logical_not(owner))
    def _():
        arrived(r_c.at[0], recv2.at[0:4])
        arrived(s_b, recv2.at[0:8])

    spread(pl.ds(0, 4))
    arrived(r_c.at[1], recv2.at[0:4])
    spread(pl.ds(4, 4))

    @pl.when(owner)
    def _():
        arrived(s_c, recv2.at[1:NZ])

    arrived(s_video, usend.at[0:3])
    arrived(s_w, w1_ref.at[:, 0:96])
    arrived(s_wc, w1_ref.at[:, 0:96])
    arrived(s_halo, vhalo)
    arrived(s_cot, coth)
    arrived(s_flag, flagh)
    arrived(s_unit, usend.at[0:3])
    arrived(s_dhalo, dsext.at[0:2])
    arrived(s_a, recv1.at[1:NQ])
    arrived(r_d, held.at[1:NQ])
    arrived(s_d, held.at[1:NQ])


def write_kernel(enc_ref, held, out_hbm, o1_hbm, o2_hbm, o1_ref, o2_ref, sems):
    copies = [
        pltpu.make_async_copy(src, dst, sems.at[i])
        for i, (src, dst) in enumerate([(enc_ref, out_hbm), (o1_ref, o1_hbm), (o2_ref, o2_hbm)])
    ]
    copies[0].start()
    shift = 10 - (lax.axis_index("tm") // NQ + 1) // 2

    def tile(piece, i):
        return held[piece, lax.rem(i + shift, 8)].astype(F32)

    for piece in range(6):
        for i in range(8):
            rows = slice(128 * (piece % 2) + 16 * i, 128 * (piece % 2) + 16 * i + 16)
            o2_ref[piece // 2, rows, :] = tile(piece, i) * (131072.0 ** -0.5)
    copies[2].start()
    for k in range(3):
        for i in range(4):
            part = tile(6 + k // 2, 4 * (k % 2) + i)
            o1_ref[k, 16 * i : 16 * i + 16, :] = part * (262144.0 ** -0.5)
    copies[1].start()
    for copy in copies:
        copy.wait()


def per_device(video, clip_start, first_conv_weight, second_conv_weight, cotangent):
    vmem = pl.BlockSpec(memory_space=pltpu.VMEM)
    hbm = pl.BlockSpec(memory_space=pltpu.HBM)
    dma = pltpu.SemaphoreType.DMA
    encoded, held = pl.pallas_call(
        kernel,
        out_shape=(
            jax.ShapeDtypeStruct((2, 128, 512), BF16),
            jax.ShapeDtypeStruct((NQ, 8, 16, 128), BF16),
        ),
        in_specs=[hbm] * 5,
        out_specs=(vmem, vmem),
        scratch_shapes=[
            pltpu.SMEM((4,), jnp.int32),
            pltpu.VMEM((3, 256, 128), BF16),
            pltpu.VMEM((3, 256, 128), BF16),
            pltpu.VMEM((2, 128, 512), BF16),
            pltpu.VMEM((4, 128, 512), BF16),
            pltpu.VMEM((2, 128, 512), BF16),
            pltpu.VMEM((2, 128, 512), BF16),
            pltpu.VMEM((16, 512), BF16),
            pltpu.VMEM((16, 512), BF16),
            pltpu.VMEM((NX, 2, 64, 512), F32),
            pltpu.VMEM((NX, 2, 64, 512), BF16),
            pltpu.VMEM((NX, 2, 64, 512), BF16),
            pltpu.VMEM((4, 256, 512), F32),
            pltpu.VMEM((4, 256, 512), BF16),
            pltpu.VMEM((8, 128, 512), BF16),
            pltpu.VMEM((NQ, 128, 128), F32),
            pltpu.VMEM((NQ, 128, 128), BF16),
            pltpu.VMEM((NQ, 128, 128), BF16),
            pltpu.VMEM((8, 16, 128), BF16),
            pltpu.VMEM((NZ, 16, 128), BF16),
            dma((5,)),
            dma((NX,)),
            dma((2,)),
            dma((23,)),
            pltpu.SemaphoreType.REGULAR((3,)),
        ],
        compiler_params=pltpu.CompilerParams(
            collective_id=0, has_side_effects=True, vmem_limit_bytes=40 * 1024 * 1024
        ),
    )(*(
        pltpu.with_memory_space_constraint(x, pltpu.HBM)
        for x in (clip_start, video, first_conv_weight.transpose(0, 2, 1), second_conv_weight, cotangent)
    ))
    encoded, first_grad, second_grad = pl.pallas_call(
        write_kernel,
        out_shape=(
            jax.ShapeDtypeStruct((2, 128, 512), BF16),
            jax.ShapeDtypeStruct((3, 64, 128), F32),
            jax.ShapeDtypeStruct((3, 256, 128), F32),
        ),
        in_specs=[vmem] * 2,
        out_specs=(hbm,) * 3,
        scratch_shapes=[pltpu.VMEM((3, 64, 128), F32), pltpu.VMEM((3, 256, 128), F32), dma((3,))],
        compiler_params=pltpu.CompilerParams(vmem_limit_bytes=8 * 1024 * 1024),
    )(*(pltpu.with_memory_space_constraint(x, pltpu.VMEM) for x in (encoded, held)))
    return encoded, first_grad.transpose(0, 2, 1), second_grad


def solution(mesh):
    in_specs = (
        P("tm", "chan", None),
        P("tm"),
        P(None, None, "chan"),
        P(None, None, "chan"),
        P("tm", "chan", None),
    )
    out_specs = (P("tm", "chan", None), P(None, None, "chan"), P(None, None, "chan"))
    return jax.shard_map(
        per_device, mesh=mesh, in_specs=in_specs, out_specs=out_specs, check_vma=False
    )
```
